32 devices in a mesh: dp: 8 (over z, y), mp: 4 (over x, core).
Axes of the slice: x: 2, y: 2, z: 4, core: 2. Of those that a mesh axis runs over, the one named last changes fastest.
Arguments:
- features: bfloat16 [8192, 9216], P('dp', 'mp'), may hold values from -18 to 18
- labels: int32 [8192], P('dp'), may hold values from 0 to 999
- noise_six: bfloat16 [73728, 4096], P('dp', 'mp'), may hold values from 0 to 1
- noise_seven: bfloat16 [32768, 4096], P('dp', 'mp'), may hold values from 0 to 1
- noise_eight: bfloat16 [32768, 1000], P(('dp', 'mp')), may hold values from 0 to 1
- w_six: float32 [9216, 4096], P('dp', 'mp'), may hold values from -0.0625 to 0.0625
- w_seven: float32 [4096, 4096], P('dp', 'mp'), may hold values from -0.125 to 0.125
- w_eight: float32 [4096, 1000], P(('mp', 'dp')), may hold values from -0.1875 to 0.1875
- m_six: float32 [9216, 4096], P('dp', 'mp'), may hold values from -2.6119556e-05 to 2.6119556e-05
- m_seven: float32 [4096, 4096], P('dp', 'mp'), may hold values from -2.6119556e-05 to 2.6119556e-05
- m_eight: float32 [4096, 1000], P(('mp', 'dp')), may hold values from -2.6119556e-05 to 2.6119556e-05
- v_six: float32 [9216, 4096], P('dp', 'mp'), may hold values from 4.2639454e-11 to 1.7055782e-10
- v_seven: float32 [4096, 4096], P('dp', 'mp'), may hold values from 4.2639454e-11 to 1.7055782e-10
- v_eight: float32 [4096, 1000], P(('mp', 'dp')), may hold values from 4.2639454e-11 to 1.7055782e-10
- biases: float32 [2, 4096], P(None, 'mp'), may hold values from -0.5 to 0.5
- bias_out: float32 [1000], replicated, may hold values from -0.5 to 0.5
- m_biases: float32 [2, 4096], P(None, 'mp'), may hold values from -5.2239113e-05 to 5.2239113e-05
- v_biases: float32 [2, 4096], P(None, 'mp'), may hold values from 1.3644626e-10 to 6.8223127e-10
- m_bias_out: float32 [1000], replicated, may hold values from -0.0002611956 to 0.0002611956
- v_bias_out: float32 [1000], replicated, may hold values from 2.1319728e-09 to 3.4111565e-08
Outputs:
- loss: float32 [], replicated
- grad_norm: float32 [], replicated
- new_six: float32 [9216, 4096], P('dp', 'mp')
- new_seven: float32 [4096, 4096], P('dp', 'mp')
- new_eight: float32 [4096, 1000], P(('mp', 'dp'))
- new_m_six: float32 [9216, 4096], P('dp', 'mp')
- new_m_seven: float32 [4096, 4096], P('dp', 'mp')
- new_m_eight: float32 [4096, 1000], P(('mp', 'dp'))
- new_v_six: float32 [9216, 4096], P('dp', 'mp')
- new_v_seven: float32 [4096, 4096], P('dp', 'mp')
- new_v_eight: float32 [4096, 1000], P(('mp', 'dp'))
- copy_six: bfloat16 [9216, 4096], P('dp', 'mp')
- copy_seven: bfloat16 [4096, 4096], P('dp', 'mp')
- copy_eight: bfloat16 [4096, 1000], P(('mp', 'dp'))
- new_biases: float32 [2, 4096], P(None, 'mp')
- new_bias_out: float32 [1000], replicated
- new_m_biases: float32 [2, 4096], P(None, 'mp')
- new_v_biases: float32 [2, 4096], P(None, 'mp')
- new_m_bias_out: float32 [1000], replicated
- new_v_bias_out: float32 [1000], replicated
The draws below stay inside these ranges and needn't reach their ends.
All inputs are finite; a program needn't handle non-finite values.
Results may differ from the reference program's by a relative error of at most 0.006.
The reference program's roundings to bfloat16 on the way count: a program that leaves them out, or rounds other values in their place, can miss the bound.
Values may be sent and summed in bfloat16 or wider, within the bound.
No kernel may reach another device: no remote copies, remote signals or barrier semaphores. Data moves between devices by JAX's collectives and lax.ppermute only.
A program may use at most 320 MiB of HBM per device.

```python
import math
import jax
import jax.numpy as jnp
from jax import lax

D_IN = 9216
H = 4096
C = 1000
B_DEV = 1024
STEP = 3
TOKENS = 8192
NPARAM = 58631144
N_DP = 8
N_MP = 4


def draw_features(key, part):
    key_base = jax.random.fold_in(key, 11)
    key_rows = jax.random.fold_in(key, 12)
    position = jnp.arange(TOKENS, dtype=jnp.float32) / max(TOKENS - 1, 1)
    trend = jnp.exp(jnp.log(3.0) * position)
    base = jnp.clip(jax.random.normal(key_base, (TOKENS, D_IN), jnp.float32), -4.0, 4.0)
    jitter = jnp.exp(jax.random.uniform(key_rows, (TOKENS, 1), jnp.float32, -0.35, 0.35))
    return (base * trend[:, None] * jitter).astype(jnp.bfloat16)


def with_ends(entries, own_key, least, high):
    longest = entries.shape.index(max(entries.shape))
    spots = []
    for shift in (0, 1):
        where = [jax.random.randint(jax.random.fold_in(own_key, axis), (), 0, length) for axis, length in enumerate(entries.shape)]
        where[longest] = (where[longest] + shift) % entries.shape[longest]
        spots.append(tuple(where))
    return entries.at[spots[0]].set(least).at[spots[1]].set(high)


def steps_of(rng, shape, shards, least, high):
    loudness = 1.0
    for dim, shards_of in shards:
        steps = jax.random.uniform(jax.random.fold_in(jax.random.fold_in(rng, 6), dim), (shards_of,), jnp.float32, least / len(shards), high / len(shards))
        loudness = loudness * jnp.repeat(jnp.exp(steps), shape[dim] // shards_of).reshape((-1,) + (1,) * (len(shape) - 1 - dim))
    return loudness


def noise(rng, shape, scale, reach, shards=(), kind=jnp.bfloat16):
    level = steps_of(rng, shape, shards, -0.22, 0.18) if shards else 1.0
    drawn = jax.random.normal(rng, shape, jnp.float32) * scale * level
    return jnp.minimum(jnp.maximum(drawn, -reach), reach).astype(kind)


def setup_inputs(seed: int = 0) -> dict:
    key_list = jax.random.split(jax.random.key(seed), 21)
    return {
        "features": draw_features(jax.random.fold_in(key_list[20], 71), 0),
        "labels": with_ends(jax.random.randint(key_list[1], (TOKENS,), 0, C), jax.random.fold_in(key_list[1], 1), 0, C - 1).astype(jnp.int32),
        "noise_six": jnp.clip(1.0 * jax.random.uniform(key_list[2], (N_DP * D_IN, H), jnp.float32) ** steps_of(key_list[2], (N_DP * D_IN, H), ((0, 8), (1, 4)), -0.2, 0.2), 0.0, 1.0).astype(jnp.bfloat16),
        "noise_seven": jnp.clip(1.0 * jax.random.uniform(key_list[3], (N_DP * H, H), jnp.float32) ** steps_of(key_list[3], (N_DP * H, H), ((0, 8), (1, 4)), -0.2, 0.2), 0.0, 1.0).astype(jnp.bfloat16),
        "noise_eight": jnp.clip(1.0 * jax.random.uniform(key_list[4], (N_DP * H, C), jnp.float32) ** steps_of(key_list[4], (N_DP * H, C), ((0, 32),), -0.2, 0.2), 0.0, 1.0).astype(jnp.bfloat16),
        "w_six": noise(key_list[5], (D_IN, H), D_IN ** -0.5, 0.0625, ((0, 8), (1, 4)), jnp.float32),
        "w_seven": noise(key_list[6], (H, H), (H // 2) ** -0.5, 0.125, ((0, 8), (1, 4)), jnp.float32),
        "w_eight": noise(key_list[7], (H, C), (H // 4) ** -0.5, 0.1875, ((0, 32),), jnp.float32),
        "m_six": noise(key_list[8], (D_IN, H), (0.05 / NPARAM ** 0.5), 2.6119556423509493e-05, ((0, 8), (1, 4)), jnp.float32),
        "m_seven": noise(key_list[9], (H, H), (0.05 / NPARAM ** 0.5), 2.6119556423509493e-05, ((0, 8), (1, 4)), jnp.float32),
        "m_eight": noise(key_list[10], (H, C), (0.05 / NPARAM ** 0.5), 2.6119556423509493e-05, ((0, 32),), jnp.float32),
        "v_six": jnp.clip(jnp.exp(math.log(1.7055781786901036e-10) - 1.3862944 * jax.random.uniform(key_list[11], (D_IN, H), jnp.float32) ** steps_of(key_list[11], (D_IN, H), ((0, 8), (1, 4)), -0.2, 0.2)), 4.263945446725259e-11, 1.7055781786901036e-10),
        "v_seven": jnp.clip(jnp.exp(math.log(1.7055781786901036e-10) - 1.3862944 * jax.random.uniform(key_list[12], (H, H), jnp.float32) ** steps_of(key_list[12], (H, H), ((0, 8), (1, 4)), -0.2, 0.2)), 4.263945446725259e-11, 1.7055781786901036e-10),
        "v_eight": jnp.clip(jnp.exp(math.log(1.7055781786901036e-10) - 1.3862944 * jax.random.uniform(key_list[13], (H, C), jnp.float32) ** steps_of(key_list[13], (H, C), ((0, 32),), -0.2, 0.2)), 4.263945446725259e-11, 1.7055781786901036e-10),
        "biases": noise(key_list[14], (2, H), 0.1, 0.5, ((1, 4),), jnp.float32),
        "bias_out": noise(key_list[15], (C,), 0.1, 0.5, (), jnp.float32),
        "m_biases": noise(key_list[16], (2, H), (0.1 / NPARAM ** 0.5), 5.223911284701899e-05, ((1, 4),), jnp.float32),
        "v_biases": jnp.clip(jnp.exp(math.log(6.822312714760415e-10) - 1.609438 * jax.random.uniform(key_list[17], (2, H), jnp.float32) ** steps_of(key_list[17], (2, H), ((1, 4),), -0.2, 0.2)), 1.3644625707076585e-10, 6.822312714760415e-10),
        "m_bias_out": noise(key_list[18], (C,), (0.5 / NPARAM ** 0.5), 0.0002611956, (), jnp.float32),
        "v_bias_out": jnp.clip(jnp.exp(jax.random.uniform(key_list[19], (C,), jnp.float32, math.log(2.131972820507144e-09), math.log(3.411156512811431e-08))), 2.131972820507144e-09, 3.411156512811431e-08),
    }


beta_one = 0.5
beta_two = 0.5
learn_rate = 0.01
bias_rate = 0.05
decay_rate = 0.1
adam_eps = 1e-08
clip_norm = 0.05
tiny_eps = 1e-12

@jax.custom_vjp
def low(v):
    return lax.optimization_barrier(v.astype(jnp.bfloat16)).astype(jnp.float32)

@jax.custom_vjp
def low_back(v):
    return v

def low_keep(v):
    return (low(v), None)

def low_pass(kept, grad):
    return (grad,)

def back_keep(v):
    return (v, None)

def back_low(kept, grad):
    return (low(grad),)
low.defvjp(low_keep, low_pass)
low_back.defvjp(back_keep, back_low)

def product(left, right):
    return jnp.dot(left, right, precision=lax.Precision.HIGHEST)

def group_loss(params, inputs, targets):
    weight_six, weight_seven, weight_eight, bias_pair, bias_last = params
    pre_six = low_back(product(inputs, low(weight_six)) + bias_pair[0])
    hidden_six = low(jax.nn.silu(pre_six))
    pre_seven = low_back(product(hidden_six, low(weight_seven)) + bias_pair[1])
    hidden_seven = low(jax.nn.silu(pre_seven))
    logits = low_back(product(hidden_seven, low(weight_eight)) + bias_last)
    log_total = jax.nn.logsumexp(logits, axis=1)
    onehot = (targets[:, None] == jnp.arange(C)[None, :]).astype(logits.dtype)
    picked = lax.optimization_barrier(jnp.sum(onehot * logits, axis=1))
    return jnp.sum(log_total - picked) / TOKENS

def column_blocks(matrix):
    return matrix.reshape(matrix.shape[0], N_MP, -1).transpose(1, 0, 2)

def column_merge(blocks):
    return blocks.transpose(1, 0, 2).reshape(blocks.shape[1], -1)

def row_blocks(matrix):
    return matrix.reshape(N_MP, -1, matrix.shape[1])

def row_merge(blocks):
    return blocks.reshape(-1, blocks.shape[2])

def block_views(items):
    return (column_blocks(items[0]), column_blocks(items[1]), row_blocks(items[2]))

def clip_blocks(blocks):
    spread = jnp.sqrt(lax.optimization_barrier(jnp.mean(blocks * blocks, axis=(1, 2), keepdims=True)))
    clipped = jnp.clip(blocks, -2.5 * spread, 2.5 * spread)
    return (clipped, lax.optimization_barrier(jnp.max(jnp.abs(clipped), axis=(1, 2))))

def soft_ternary(clipped, peak_val, noise_val):
    ratio = clipped / (peak_val + tiny_eps)
    value = jnp.clip(4.0 * ratio, -1.0, 1.0) * jnp.clip(2.0 * (jnp.abs(ratio) - noise_val) + 0.5, 0.0, 1.0)
    return lax.optimization_barrier(value.astype(jnp.bfloat16)).astype(jnp.float32)

def adam_step(weight, moment, second, grad_val, decay, rate):
    moment_new = beta_one * moment + (1.0 - beta_one) * grad_val
    second_new = beta_two * second + (1.0 - beta_two) * grad_val * grad_val
    first_fix = 1.0 - beta_one ** STEP
    second_fix = 1.0 - beta_two ** STEP
    weight_new = weight - rate * (moment_new / first_fix / (jnp.sqrt(second_new / second_fix) + adam_eps) + decay * weight)
    return (weight_new, moment_new, second_new)

def reference(features, labels, noise_six, noise_seven, noise_eight, w_six, w_seven, w_eight, m_six, m_seven, m_eight, v_six, v_seven, v_eight, biases, bias_out, m_biases, v_biases, m_bias_out, v_bias_out):
    params = (w_six, w_seven, w_eight, biases, bias_out)
    inputs = features.astype(jnp.float32).reshape(N_DP, B_DEV, D_IN)
    targets = labels.reshape(N_DP, B_DEV)

    def gradients(inputs_one, targets_one):
        loss_part, pullback = jax.vjp(lambda values: group_loss(values, inputs_one, targets_one), params)
        return (loss_part, pullback(jnp.ones_like(loss_part))[0])

    def first_pass(group_data):
        loss_part, grads = gradients(group_data[0], group_data[1])
        return tuple((clip_blocks(block)[1] for block in block_views(grads)))
    maxima = lax.map(first_pass, (inputs, targets))
    maxima = tuple((lax.optimization_barrier(jnp.max(item, axis=0)) for item in maxima))
    noise_views = (noise_six.reshape(N_DP, D_IN, H), noise_seven.reshape(N_DP, H, H), noise_eight.reshape(N_DP, H, C))

    def second_pass(carried, group_data):
        loss_part, grads = gradients(group_data[0], group_data[1])
        noise_blocks = block_views(tuple((item.astype(jnp.float32) for item in group_data[2:])))
        ternary = tuple((soft_ternary(clip_blocks(block)[0], peak_val[:, None, None], noise_val) for block, peak_val, noise_val in zip(block_views(grads), maxima, noise_blocks)))
        summed = tuple((old + new for old, new in zip(carried[0], ternary)))
        return ((summed, carried[1] + grads[3], carried[2] + grads[4], carried[3] + loss_part), None)
    start = ((jnp.zeros((N_MP, D_IN, H // N_MP), jnp.float32), jnp.zeros((N_MP, H, H // N_MP), jnp.float32), jnp.zeros((N_MP, H // N_MP, C), jnp.float32)), jnp.zeros((2, H), jnp.float32), jnp.zeros((C,), jnp.float32), jnp.zeros((), jnp.float32))
    carried, unused = lax.scan(second_pass, start, (inputs, targets) + noise_views)
    summed, grad_pair, grad_last, loss = carried
    scaled = tuple((peak_val[:, None, None] * block for peak_val, block in zip(maxima, summed)))
    reduced = (column_merge(scaled[0]), column_merge(scaled[1]), row_merge(scaled[2]))
    squares = sum((jnp.sum(item * item) for item in reduced)) + jnp.sum(grad_pair * grad_pair) + jnp.sum(grad_last * grad_last)
    grad_norm = jnp.sqrt(squares)
    factor = clip_norm / jnp.maximum(grad_norm, clip_norm)
    new_six, new_m_six, new_v_six = adam_step(w_six, m_six, v_six, factor * reduced[0], decay_rate, learn_rate)
    new_seven, new_m_seven, new_v_seven = adam_step(w_seven, m_seven, v_seven, factor * reduced[1], decay_rate, learn_rate)
    new_eight, new_m_eight, new_v_eight = adam_step(w_eight, m_eight, v_eight, factor * reduced[2], decay_rate, learn_rate)
    new_biases, new_m_biases, new_v_biases = adam_step(biases, m_biases, v_biases, factor * grad_pair, 0.0, bias_rate)
    new_bias_out, new_m_bias_out, new_v_bias_out = adam_step(bias_out, m_bias_out, v_bias_out, factor * grad_last, 0.0, bias_rate)
    return (loss, grad_norm, new_six, new_seven, new_eight, new_m_six, new_m_seven, new_m_eight, new_v_six, new_v_seven, new_v_eight, new_six.astype(jnp.bfloat16), new_seven.astype(jnp.bfloat16), new_eight.astype(jnp.bfloat16), new_biases, new_bias_out, new_m_biases, new_v_biases, new_m_bias_out, new_v_bias_out)
```

```python
import jax
import jax.numpy as jnp
from jax import lax
from jax.sharding import PartitionSpec as P

STEP = 3


beta_one = 0.5
beta_two = 0.5
learn_rate = 0.01
bias_rate = 0.05
decay_rate = 0.1
adam_eps = 1e-08
clip_norm = 0.05
tiny_eps = 1e-12


def matmul(left, right):
    return jnp.dot(left, right, preferred_element_type=jnp.float32)


def contract_rows(left, right):
    return lax.dot_general(
        left, right, (((0,), (0,)), ((), ())), preferred_element_type=jnp.float32
    )


def against_rows(left, right):
    return lax.dot_general(
        left, right, (((1,), (1,)), ((), ())), preferred_element_type=jnp.float32
    )


def layer_forward(pre_sum, bias_row):
    pre_act = pre_sum + bias_row
    return (pre_act, jax.nn.silu(pre_act).astype(jnp.bfloat16))


def layer_delta(pre_act, upstream):
    sigmoid_val = jax.nn.sigmoid(pre_act)
    slope = sigmoid_val * (1.0 + pre_act * (1.0 - sigmoid_val))
    return (upstream * slope).astype(jnp.bfloat16)


def grad_limits(grad_block):
    limit = 2.5 * jnp.sqrt(jnp.mean(grad_block * grad_block))
    return (limit, jnp.minimum(jnp.max(jnp.abs(grad_block)), limit))


def swap(value, axis, bit):
    size = lax.axis_size(axis)
    return lax.ppermute(value, axis, [(i, i ^ bit) for i in range(size)])


def turn(value):
    size = lax.axis_size("dp")
    return lax.ppermute(value, "dp", [(i, (i + 2) % size) for i in range(size)])


def spread_bits(axis):
    bit = 1
    while bit < lax.axis_size(axis):
        yield bit
        bit *= 2


def fold(value, combine, axes):
    for axis in axes:
        for bit in spread_bits(axis):
            value = combine(value, swap(value, axis, bit))
    return value


def after(value, *earlier):
    return lax.optimization_barrier((value, earlier))[0]


def place(row, block_rows):
    if block_rows is None:
        return row
    mine = lax.axis_index("mp")
    return ((row // block_rows) ^ mine) * block_rows + row % block_rows


def owner(step, flip):
    size = lax.axis_size("dp")
    here = lax.axis_index("dp")
    return ((here + size - 2 * step) % size) ^ flip


def put(whole, piece, row):
    return lax.dynamic_update_slice(whole, piece, (row, 0))


def take(whole, row, rows):
    return lax.dynamic_slice_in_dim(whole, row, rows, 0)


def xor_columns(value):
    blocks = {0: value}
    for bit in reversed(list(spread_bits("mp"))):
        blocks |= {step ^ bit: swap(item, "mp", bit) for step, item in blocks.items()}
    return jnp.concatenate([blocks[step] for step in sorted(blocks)], axis=1)


def soft_ternary(grad_block, limit, peak_val, noise_val):
    clipped = jnp.clip(grad_block, -limit, limit)
    ratio = clipped / (peak_val + tiny_eps)
    value = jnp.clip(4.0 * ratio, -1.0, 1.0) * jnp.clip(
        2.0 * (jnp.abs(ratio) - noise_val.astype(jnp.float32)) + 0.5, 0.0, 1.0
    )
    return value.astype(jnp.bfloat16)


def adam_step(weight, moment, second, grad_val, decay, rate):
    moment_new = beta_one * moment + (1.0 - beta_one) * grad_val
    second_new = beta_two * second + (1.0 - beta_two) * grad_val * grad_val
    first_fix = 1.0 - beta_one**STEP
    second_fix = 1.0 - beta_two**STEP
    weight_new = weight - rate * (
        moment_new / first_fix / (jnp.sqrt(second_new / second_fix) + adam_eps) + decay * weight
    )
    return (weight_new, moment_new, second_new)


def shards(
    features,
    labels,
    noise_six,
    noise_seven,
    noise_eight,
    w_six,
    w_seven,
    w_eight,
    m_six,
    m_seven,
    m_eight,
    v_six,
    v_seven,
    v_eight,
    biases,
    bias_out,
    m_biases,
    v_biases,
    m_bias_out,
    v_bias_out,
):
    mine = lax.axis_index("mp")
    here = lax.axis_index("dp")
    replicas = lax.axis_size("dp")
    ways = lax.axis_size("mp")
    rings = replicas // 2
    batch_rows = features.shape[0]
    tokens = batch_rows * replicas
    part_rows = batch_rows // ways

    def gather(shard, block_rows):
        rows = shard.shape[0]
        whole = jnp.zeros((rows * replicas, shard.shape[1]), shard.dtype)
        for step in range(rings):
            other = swap(shard, "dp", 1)
            whole = put(whole, shard, place(owner(step, 0) * rows, block_rows))
            whole = put(whole, other, place(owner(step, 1) * rows, block_rows))
            last = shard
            if step < rings - 1:
                shard = turn(shard)
        return whole, last

    cast_six = w_six.astype(jnp.bfloat16)
    cast_seven = w_seven.astype(jnp.bfloat16)
    cast_eight = w_eight.astype(jnp.bfloat16)
    inputs = xor_columns(features)
    kept_six, last_six = gather(cast_six, features.shape[1])
    cast_seven = after(cast_seven, last_six)
    kept_seven, last_seven = gather(cast_seven, biases.shape[1])
    cast_eight = after(cast_eight, last_seven)
    kept_eight, _ = gather(cast_eight, None)
    pre_six, out_six = layer_forward(matmul(inputs, kept_six), biases[0])
    hidden = xor_columns(out_six)
    pre_seven, out_seven = layer_forward(matmul(hidden, kept_seven), biases[1])

    def part(step):
        return matmul(take(out_seven, (mine ^ step) * part_rows, part_rows), kept_eight)

    parts = {step: part(step) for step in range(ways)}
    for bit in spread_bits("mp"):
        for step in range(0, ways, 2 * bit):
            parts[step] = parts[step] + swap(parts[step + bit], "mp", bit)
    logits = parts[0] + bias_out
    labels_part = lax.dynamic_slice_in_dim(labels, mine * part_rows, part_rows, 0)
    top_logit = jnp.max(logits, axis=1, keepdims=True)
    shifted = jnp.exp(logits - top_logit)
    row_total = jnp.sum(shifted, axis=1, keepdims=True)
    log_total = top_logit[:, 0] + jnp.log(row_total[:, 0])
    classes = lax.broadcasted_iota(jnp.int32, logits.shape, 1)
    onehot = (classes == labels_part[:, None]).astype(jnp.float32)
    loss_part = jnp.sum(log_total - jnp.sum(onehot * logits, axis=1)) / tokens
    dz_part = ((shifted / row_total - onehot) / tokens).astype(jnp.bfloat16)
    dz_parts = [dz_part]
    for bit in spread_bits("mp"):
        dz_parts = dz_parts + [swap(item, "mp", bit) for item in dz_parts]
    dlogits = jnp.zeros((batch_rows, logits.shape[1]), jnp.bfloat16)
    for step, item in enumerate(dz_parts):
        dlogits = put(dlogits, item, (mine ^ step) * part_rows)

    delta_seven = layer_delta(pre_seven, against_rows(dlogits, kept_eight))
    width = biases.shape[1]
    ups = {
        step: against_rows(delta_seven, kept_seven[step * width : (step + 1) * width])
        for step in range(ways)
    }
    for bit in spread_bits("mp"):
        for step in range(0, ways, 2 * bit):
            ups[step] = ups[step] + swap(ups[step + bit], "mp", bit)
    delta_six = layer_delta(pre_six, ups[0])
    grad_eight = contract_rows(out_seven, dlogits)
    grad_seven = contract_rows(hidden, delta_seven)
    limit_seven, peak_seven = grad_limits(grad_seven)
    limit_eight, peak_eight = grad_limits(grad_eight)
    tops = fold(jnp.stack([peak_seven, peak_eight]), jnp.maximum, ("dp",))
    top_seven, top_eight = tops[0], tops[1]
    grad_six = contract_rows(inputs, delta_six)
    limit_six, peak_six = grad_limits(grad_six)
    top_six = fold(peak_six, jnp.maximum, ("dp",))

    def reduce(grad, limit, top, noise, rows, block_rows, hold):
        def tern(step, flip):
            row = owner(step, flip) * rows
            return soft_ternary(
                take(grad, place(row, block_rows), rows), limit, top, take(noise, row, rows)
            )

        total = None
        first = None
        for step in list(range(1, rings)) + [0]:
            away = tern(step, 1)
            if hold is not None:
                away = after(away, hold)
            near = swap(away, "dp", 1)
            pair = tern(step, 0).astype(jnp.float32) + near.astype(jnp.float32)
            if total is not None:
                pair = pair + turn(total).astype(jnp.float32)
            total = pair.astype(jnp.bfloat16)
            first = near if step == rings - 1 else first
        return top * pair, first

    reduced_eight, mark = reduce(
        grad_eight, limit_eight, top_eight, noise_eight, w_eight.shape[0], None, None
    )
    reduced_seven, mark = reduce(
        grad_seven, limit_seven, top_seven, noise_seven, w_seven.shape[0], width, None
    )
    reduced_six, mark = reduce(
        grad_six, limit_six, top_six, noise_six, w_six.shape[0], features.shape[1], None
    )
    bias_sums = fold(
        jnp.concatenate(
            [
                jnp.sum(delta_six.astype(jnp.float32), axis=0),
                jnp.sum(delta_seven.astype(jnp.float32), axis=0),
                jnp.sum(dlogits.astype(jnp.float32), axis=0),
            ]
        ),
        jnp.add,
        ("dp",),
    )
    grad_pair = bias_sums[: 2 * width].reshape(2, width)
    grad_out = bias_sums[2 * width :]
    squares = (
        jnp.sum(reduced_six * reduced_six)
        + jnp.sum(reduced_seven * reduced_seven)
        + jnp.sum(reduced_eight * reduced_eight)
        + jnp.sum(grad_pair * grad_pair) / replicas
        + jnp.sum(grad_out * grad_out) / (replicas * ways)
    )
    totals = fold(jnp.stack([squares, loss_part]), jnp.add, ("dp", "mp"))
    total_squares, loss = totals[0], totals[1]
    grad_norm = jnp.sqrt(total_squares)
    factor = clip_norm / jnp.maximum(grad_norm, clip_norm)
    new_six, new_m_six, new_v_six = adam_step(
        w_six, m_six, v_six, factor * reduced_six, decay_rate, learn_rate
    )
    new_seven, new_m_seven, new_v_seven = adam_step(
        w_seven, m_seven, v_seven, factor * reduced_seven, decay_rate, learn_rate
    )
    new_eight, new_m_eight, new_v_eight = adam_step(
        w_eight, m_eight, v_eight, factor * reduced_eight, decay_rate, learn_rate
    )
    new_biases, new_m_biases, new_v_biases = adam_step(
        biases, m_biases, v_biases, factor * grad_pair, 0.0, bias_rate
    )
    new_bias_out, new_m_bias_out, new_v_bias_out = adam_step(
        bias_out, m_bias_out, v_bias_out, factor * grad_out, 0.0, bias_rate
    )
    return (
        loss,
        grad_norm,
        new_six,
        new_seven,
        new_eight,
        new_m_six,
        new_m_seven,
        new_m_eight,
        new_v_six,
        new_v_seven,
        new_v_eight,
        new_six.astype(jnp.bfloat16),
        new_seven.astype(jnp.bfloat16),
        new_eight.astype(jnp.bfloat16),
        new_biases,
        new_bias_out,
        new_m_biases,
        new_v_biases,
        new_m_bias_out,
        new_v_bias_out,
    )


def solution(mesh):
    return jax.shard_map(
        shards,
        mesh=mesh,
        in_specs=(
            P("dp", "mp"),
            P("dp"),
            P("dp", "mp"),
            P("dp", "mp"),
            P(("dp", "mp"), None),
            P("dp", "mp"),
            P("dp", "mp"),
            P(("mp", "dp"), None),
            P("dp", "mp"),
            P("dp", "mp"),
            P(("mp", "dp"), None),
            P("dp", "mp"),
            P("dp", "mp"),
            P(("mp", "dp"), None),
            P(None, "mp"),
            P(),
            P(None, "mp"),
            P(None, "mp"),
            P(),
            P(),
        ),
        out_specs=(
            P(),
            P(),
            P("dp", "mp"),
            P("dp", "mp"),
            P(("mp", "dp"), None),
            P("dp", "mp"),
            P("dp", "mp"),
            P(("mp", "dp"), None),
            P("dp", "mp"),
            P("dp", "mp"),
            P(("mp", "dp"), None),
            P("dp", "mp"),
            P("dp", "mp"),
            P(("mp", "dp"), None),
            P(None, "mp"),
            P(),
            P(None, "mp"),
            P(None, "mp"),
            P(),
            P(),
        ),
        check_vma=False,
    )
```

```python
import jax
import jax.numpy as jnp
from jax import lax
from jax.sharding import PartitionSpec as P

STEP = 3


beta_one = 0.5
beta_two = 0.5
learn_rate = 0.01
bias_rate = 0.05
decay_rate = 0.1
adam_eps = 1e-08
clip_norm = 0.05
tiny_eps = 1e-12


def matmul(left, right):
    return jnp.dot(left, right, preferred_element_type=jnp.float32)


def contract_rows(left, right):
    return lax.dot_general(
        left, right, (((0,), (0,)), ((), ())), preferred_element_type=jnp.float32
    )


def against_rows(left, right):
    return lax.dot_general(
        left, right, (((1,), (1,)), ((), ())), preferred_element_type=jnp.float32
    )


def layer_forward(pre_sum, bias_row):
    pre_act = pre_sum + bias_row
    return (pre_act, jax.nn.silu(pre_act).astype(jnp.bfloat16))


def layer_delta(pre_act, upstream):
    sigmoid_val = jax.nn.sigmoid(pre_act)
    slope = sigmoid_val * (1.0 + pre_act * (1.0 - sigmoid_val))
    return (upstream * slope).astype(jnp.bfloat16)


def grad_limits(grad_block, columns):
    squares = jnp.sum(grad_block * grad_block)
    limit = 2.5 * jnp.sqrt(squares / (grad_block.shape[0] * columns))
    return (limit, jnp.minimum(jnp.max(jnp.abs(grad_block)), limit))


def swap(value, axis, bit):
    size = lax.axis_size(axis)
    return lax.ppermute(value, axis, [(i, i ^ bit) for i in range(size)])


def turn(value):
    size = lax.axis_size("dp")
    return lax.ppermute(value, "dp", [(i, (i + 2) % size) for i in range(size)])


def spread_bits(axis):
    bit = 1
    while bit < lax.axis_size(axis):
        yield bit
        bit *= 2


def fold(value, combine, axes):
    for axis in axes:
        for bit in spread_bits(axis):
            value = combine(value, swap(value, axis, bit))
    return value


def settle(*values):
    return lax.optimization_barrier(values)


def owner(step, flip):
    size = lax.axis_size("dp")
    here = lax.axis_index("dp")
    return ((here + size - 2 * step) % size) ^ flip


def place(index, blocks):
    if blocks is None:
        return index
    mine = lax.axis_index("mp")
    return ((index // blocks) ^ mine) * blocks + index % blocks


def put(whole, piece, index, row=0):
    return lax.dynamic_update_slice(whole, piece[None], (index, row, 0))


def take(whole, index, row, rows):
    return lax.dynamic_slice(whole, (index, row, 0), (1, rows, whole.shape[2]))[0]


def xor_blocks(value, bits):
    blocks = {0: value}
    for bit in bits:
        blocks |= {step ^ bit: swap(item, "mp", bit) for step, item in blocks.items()}
    return blocks


def near_rows(rows, rings):
    return max(16, (rows // (2 * rings + 2) + 8) // 16 * 16)


def reorder(whole, group):
    if group is None:
        return whole
    mine = lax.axis_index("mp")
    ways = whole.shape[0] // group
    grouped = whole.reshape(ways, group, *whole.shape[1:])
    return jnp.concatenate(
        [lax.dynamic_index_in_dim(grouped, mine ^ step, 0, keepdims=False) for step in range(ways)]
    )


def overlaps(sizes, row, count):
    start = 0
    for spot, size in enumerate(sizes):
        low, high = max(row, start), min(row + count, start + size)
        if low < high:
            yield spot, low - start, high - low, low - row
        start += size


def soft_ternary(grad_block, limit, peak_val, noise_val):
    clipped = jnp.clip(grad_block, -limit, limit)
    ratio = clipped / (peak_val + tiny_eps)
    value = jnp.clip(4.0 * ratio, -1.0, 1.0) * jnp.clip(
        2.0 * (jnp.abs(ratio) - noise_val.astype(jnp.float32)) + 0.5, 0.0, 1.0
    )
    return value.astype(jnp.bfloat16)


def adam_step(weight, moment, second, grad_val, decay, rate):
    moment_new = beta_one * moment + (1.0 - beta_one) * grad_val
    second_new = beta_two * second + (1.0 - beta_two) * grad_val * grad_val
    first_fix = 1.0 - beta_one**STEP
    second_fix = 1.0 - beta_two**STEP
    weight_new = weight - rate * (
        moment_new / first_fix / (jnp.sqrt(second_new / second_fix) + adam_eps) + decay * weight
    )
    return (weight_new, moment_new, second_new)


LONG_RING = 8


def spans_of(rows, count):
    marks = [rows * i // count // 16 * 16 for i in range(count)] + [rows]
    return list(zip(marks[:-1], marks[1:]))


def same(carried):
    return carried


def gather(shards, groups, near, beside, carried):
    rings = lax.axis_size("dp") // 2
    if rings > LONG_RING:
        wholes = [lax.all_gather(shard, "dp", axis=0) for shard in shards]
        for work in beside:
            carried = work(carried)
        return [reorder(whole, group) for whole, group in zip(wholes, groups)], carried
    beside = beside + [same] * (2 * rings - len(beside))
    sizes = [shard.shape[0] for shard in shards]
    shard = jnp.concatenate(shards) if len(shards) > 1 else shards[0]
    cut = shard.shape[0] - near
    far, pair = shard[:cut], shard[cut:]

    def store(wholes, piece, step, flip, row):
        wholes = list(wholes)
        for spot, inner, count, outer in overlaps(sizes, row, piece.shape[0]):
            index = place(owner(step, flip), groups[spot])
            wholes[spot] = put(wholes[spot], piece[outer : outer + count], index, inner)
        return wholes

    wholes = [jnp.zeros((2 * rings, *item.shape), item.dtype) for item in shards]
    for step in range(rings - 1):
        other = swap(far, "dp", 1)
        if step == 0 and near:
            pair = [pair, swap(pair, "dp", 1)]
        moved = turn(far)
        carried = beside[step](carried)
        if step == 0:
            other, pair, moved, carried, shard = settle(other, pair, moved, carried, shard)
            wholes = store(wholes, shard, 0, 0, 0)
            if near:
                wholes = store(wholes, pair[1], 0, 1, cut)
        else:
            other, pair, moved, carried, wholes = settle(other, pair, moved, carried, wholes)
        wholes = store(wholes, other, step, 1, 0)
        wholes = store(wholes, moved, step + 1, 0, 0)
        far = moved
    pair = jnp.concatenate(pair) if near else None
    for hop, (low, high) in enumerate(spans_of(cut, rings - 1 if near else 1), 1):
        other = swap(far[low:high], "dp", 1)
        pair = turn(pair) if near else None
        carried = beside[rings - 2 + hop](carried)
        other, pair, far, carried, wholes = settle(other, pair, far, carried, wholes)
        wholes = store(wholes, other, rings - 1, 1, low)
        for flip in (0, 1) if near else ():
            wholes = store(wholes, pair[flip * near : (flip + 1) * near], hop, flip, cut)
    return wholes, carried


def scatter(grads, limits, tops, noises, groups, nears, ahead, beside, carried):
    rings = lax.axis_size("dp") // 2
    if rings > LONG_RING:
        for work in beside:
            carried = work(carried)
        results = []
        for grad, limit, top, noise, group in zip(grads, limits, tops, noises, groups):
            tern = soft_ternary(reorder(grad, group), limit, top, noise)
            total = lax.psum_scatter(tern.astype(jnp.float32), "dp", scatter_dimension=0)
            results.append(top * total)
        return results, carried
    beside = beside + [same] * (2 * rings - len(beside))
    spots = range(len(grads))
    cuts = [grad.shape[1] - near for grad, near in zip(grads, nears)]
    hops = rings - 1 if any(nears) else 1
    cutting = [
        spans_of(cut, hops) if near else [(0, cut)] + [None] * (hops - 1)
        for cut, near in zip(cuts, nears)
    ]

    ready = [
        soft_ternary(grad, limit, top, noise) if group is None else None
        for grad, limit, top, noise, group in zip(grads, limits, tops, noises, groups)
    ]

    def tern(spot, step, flip, row, count):
        index = owner(step, flip)
        if ready[spot] is not None:
            return take(ready[spot], index, row, count)
        return soft_ternary(
            take(grads[spot], place(index, groups[spot]), row, count),
            limits[spot],
            tops[spot],
            take(noises[spot], index, row, count),
        )

    def terns(step, flip, spans):
        return [
            None if span is None else tern(spot, step, flip, span[0], span[1] - span[0])
            for spot, span in zip(spots, spans)
        ]

    def far_terns(step, flip):
        return terns(step, flip, [(0, cut) for cut in cuts])

    def near_terns(step):
        return [
            jnp.concatenate([tern(spot, step, flip, cuts[spot], nears[spot]) for flip in (0, 1)])
            if nears[spot]
            else None
            for spot in spots
        ]

    def each(work, *lists):
        return [None if items[0] is None else work(*items) for items in zip(*lists)]

    def wide(value):
        return value.astype(jnp.float32)

    def narrow(value):
        return value.astype(jnp.bfloat16)

    def across(value):
        return swap(value, "dp", 1)

    order = list(range(1, rings)) + [0]
    pairs = near_terns(order[0])
    sending = [terns(order[0], 1, [cut[0] for cut in cutting])]
    pairs, sending, limits, carried, ready = settle(pairs, sending, limits, carried, ready)
    aways, owns = {}, {}
    got = [[] for spot in spots]
    for hop in range(1, hops + 1):
        others = each(across, sending[hop - 1])
        arrived = each(lambda item: turn(narrow(item)), pairs)
        more = near_terns(order[hop])
        if hop < hops:
            sending.append(terns(order[0], 1, [cut[hop] for cut in cutting]))
        if hop == 1:
            owns[0] = far_terns(order[0], 0)
        if hop == hops:
            aways[1] = far_terns(order[1], 1)
        carried = beside[hop - 1](carried)
        others, arrived, more, sending, aways, owns, limits, carried = settle(
            others, arrived, more, sending, aways, owns, limits, carried
        )
        pairs = each(lambda item, add: wide(item) + wide(add), arrived, more)
        for spot in spots:
            if others[spot] is not None:
                got[spot].append(others[spot])
    sums = [wide(owns[0][spot]) + wide(jnp.concatenate(got[spot])) for spot in spots]
    for spin in range(1, rings):
        others = each(across, aways[spin])
        moved = each(lambda item: turn(narrow(item)), sums)
        lasts = None
        if spin == rings - 1:
            lasts = [
                item if item is None else across(narrow(item[near:]))
                for item, near in zip(pairs, nears)
            ]
        for later in range(spin, rings if ahead else spin + 1):
            if later not in owns:
                owns[later] = far_terns(order[later], 0)
        for later in range(spin + 1, rings if ahead else min(spin + 2, rings)):
            if later not in aways:
                aways[later] = far_terns(order[later], 1)
        carried = beside[hops - 1 + spin](carried)
        others, moved, lasts, pairs, aways, owns, limits, carried = settle(
            others, moved, lasts, pairs, aways, owns, limits, carried
        )
        sums = each(
            lambda own, item, more: wide(own) + wide(item) + wide(more), owns[spin], others, moved
        )
    results = []
    for spot, near in zip(spots, nears):
        total = sums[spot]
        if near:
            total = jnp.concatenate([total, pairs[spot][:near] + wide(lasts[spot])])
        results.append(tops[spot] * total)
    return results, carried


def shards(
    features,
    labels,
    noise_six,
    noise_seven,
    noise_eight,
    w_six,
    w_seven,
    w_eight,
    m_six,
    m_seven,
    m_eight,
    v_six,
    v_seven,
    v_eight,
    biases,
    bias_out,
    m_biases,
    v_biases,
    m_bias_out,
    v_bias_out,
):
    mine = lax.axis_index("mp")
    replicas = lax.axis_size("dp")
    ways = lax.axis_size("mp")
    rings = replicas // 2
    batch_rows = features.shape[0]
    tokens = batch_rows * replicas
    half = batch_rows // 2
    width = biases.shape[1]
    outs = bias_out.shape[0]
    padded = outs + -outs % 128
    rows_six, rows_seven, rows_eight = w_six.shape[0], w_seven.shape[0], w_eight.shape[0]
    group_six, group_seven = features.shape[1] // rows_six, width // rows_seven
    near_six = near_rows(rows_six, rings)
    near_seven = near_rows(rows_seven + rows_eight, rings)
    bits = list(reversed(list(spread_bits("mp"))))
    far_bits, near_bit = bits[:-1], bits[-1]

    def widen(value):
        return jnp.pad(value, ((0, 0), (0, padded - outs)))

    def halves(value):
        return [value[:half], value[half:]]

    def over_far(own):
        done = xor_blocks(own, far_bits)
        del done[0]
        return done

    def over_near(blocks):
        return {step ^ near_bit: swap(item, "mp", near_bit) for step, item in blocks.items()}

    def join(halves_of_blocks):
        return jnp.concatenate(
            [
                jnp.concatenate([blocks[step] for step in range(ways)], axis=1)
                for blocks in halves_of_blocks
            ]
        )

    far_features = over_far(features)
    (kept_six,), (inputs, noise_wide) = gather(
        [w_six.astype(jnp.bfloat16)],
        [group_six],
        near_six,
        [
            same,
            lambda carried: swap(features, "mp", near_bit),
            lambda carried: (carried, far_features, widen(noise_eight)),
            lambda carried: carried + (over_near(carried[1]),),
            lambda carried: (
                join([{0: features, near_bit: carried[0]} | carried[1] | carried[3]]),
                carried[2],
            ),
        ],
        None,
    )

    def fc_six(carried):
        inputs, kept = carried
        pre_six, out_six = layer_forward(matmul(inputs, kept.reshape(-1, width)), biases[0])
        return (inputs, pre_six, [{0: item} for item in halves(out_six)])

    def far_half(step):
        def work(carried):
            inputs, pre_six, blocks = carried
            got = [dict(item) for item in blocks]
            got[step] |= over_far(blocks[step][0])
            for item in (0, 1):
                source = {} if item == step else {0: blocks[item][0]}
                if item < step:
                    source = {key: value for key, value in blocks[item].items() if key ^ near_bit not in blocks[item]}
                elif item > step:
                    source = {}
                got[item] |= over_near(source)
            return (inputs, pre_six, got)

        return work

    def near_half(carried):
        inputs, pre_six, blocks = carried
        got = [dict(item) for item in blocks]
        got[1] |= over_near(dict(blocks[1]))
        return (inputs, pre_six, got)

    kept_six, inputs, cast_eight, cast_seven = settle(
        kept_six, inputs, widen(w_eight.astype(jnp.bfloat16)), w_seven.astype(jnp.bfloat16)
    )
    (kept_eight, kept_seven), (inputs, pre_six, hidden_blocks) = gather(
        [cast_eight, cast_seven],
        [None, group_seven],
        near_seven,
        [fc_six, far_half(0), far_half(1), near_half],
        (inputs, kept_six),
    )
    kept_seven, kept_eight = kept_seven.reshape(-1, width), kept_eight.reshape(-1, padded)

    bias_wide = jnp.pad(bias_out, (0, padded - outs), constant_values=-1e30)
    share = half // ways

    def half_forward(number):
        pre, out = layer_forward(matmul(join([hidden_blocks[number]]), kept_seven), biases[1])
        shares = out.reshape(ways, share, width)
        parts = {
            step: matmul(lax.dynamic_index_in_dim(shares, mine ^ step, 0, keepdims=False), kept_eight)
            for step in range(ways)
        }
        for bit in reversed(bits):
            for step in range(0, ways, 2 * bit):
                parts[step] = parts[step] + swap(parts[step + bit], "mp", bit)
        logits = parts[0] + bias_wide
        labels_part = lax.dynamic_slice_in_dim(labels, number * half + mine * share, share, 0)
        top_logit = jnp.max(logits, axis=1, keepdims=True)
        shifted = jnp.exp(logits - top_logit)
        row_total = jnp.sum(shifted, axis=1, keepdims=True)
        log_total = top_logit[:, 0] + jnp.log(row_total[:, 0])
        classes = lax.broadcasted_iota(jnp.int32, logits.shape, 1)
        onehot = (classes == labels_part[:, None]).astype(jnp.float32)
        loss_part = jnp.sum(log_total - jnp.sum(onehot * logits, axis=1)) / tokens
        dz_part = ((shifted / row_total - onehot) / tokens).astype(jnp.bfloat16)
        dlogits = jnp.zeros((ways, share, padded), jnp.bfloat16)
        for step, item in xor_blocks(dz_part, bits).items():
            dlogits = put(dlogits, item, mine ^ step)
        return pre, out, dlogits.reshape(half, padded), loss_part

    both = [half_forward(number) for number in (0, 1)]
    pre_seven, out_seven, dlogits = (
        jnp.concatenate([item[spot] for item in both]) for spot in range(3)
    )
    loss_part = both[0][3] + both[1][3]
    hidden = join(hidden_blocks)

    delta_seven = layer_delta(pre_seven, against_rows(dlogits, kept_eight))

    def upstream(delta, step):
        return against_rows(delta, kept_seven[step * width : (step + 1) * width])

    top_bit = bits[0]
    cuts = [0, batch_rows // 64 * 22, batch_rows // 64 * 43, batch_rows]

    def near_sums(first, delta):
        ups = {step: upstream(delta, step) for step in range(first, first + top_bit)}
        for bit in reversed(bits[1:]):
            for step in range(first, first + top_bit, 2 * bit):
                ups[step] = ups[step] + swap(ups[step + bit], "mp", bit)
        return ups[first]

    crossing = near_sums(top_bit, delta_seven)
    grad_eight = contract_rows(out_seven, dlogits)
    limit_eight, peak_eight = grad_limits(grad_eight, outs)
    crossing, grad_eight, limit_eight, peak_eight, delta_seven, dlogits = settle(
        crossing, grad_eight, limit_eight, peak_eight, delta_seven, dlogits
    )
    crossing = [crossing[low:high] for low, high in zip(cuts[:-1], cuts[1:])]
    grad_seven = contract_rows(hidden, delta_seven)
    limit_seven, peak_seven = grad_limits(grad_seven, width)
    tops = fold(jnp.stack([peak_eight, peak_seven]), jnp.maximum, ("dp",))
    crossing, grad_seven, limit_seven, tops, delta_seven = settle(
        crossing, grad_seven, limit_seven, tops, delta_seven
    )
    top_eight, top_seven = tops[0], tops[1]

    def cross(step):
        def work(carried):
            delta, crossing, crossed, own_up = carried
            if step == 0:
                own_up = near_sums(0, delta)
            return (delta, crossing, crossed + [swap(crossing[step], "mp", top_bit)], own_up)

        return work

    def grad_fc_six(carried):
        _, _, crossed, own_up = carried
        delta_six = layer_delta(pre_six, own_up + jnp.concatenate(crossed))
        grad_six = contract_rows(inputs, delta_six)
        limit_six, peak_six = grad_limits(grad_six, width)
        return (delta_six, grad_six, limit_six, peak_six)

    def sum_or_max(one, two):
        return jnp.concatenate([one[:-1] + two[:-1], jnp.maximum(one[-1:], two[-1:])])

    def small_sums(carried):
        delta_six, grad_six, limit_six, peak_six = carried
        columns = [
            jnp.sum(item.astype(jnp.float32), axis=0) for item in (delta_six, delta_seven, dlogits)
        ]
        small = fold(jnp.concatenate(columns + [peak_six[None]]), sum_or_max, ("dp",))
        return (grad_six, limit_six, small)

    beside = [
        cross(0),
        cross(1),
        cross(2),
        grad_fc_six,
    ]
    (reduced_eight, reduced_seven), carried = scatter(
        [grad_eight.reshape(replicas, rows_eight, padded), grad_seven.reshape(replicas, rows_seven, width)],
        [limit_eight, limit_seven],
        [top_eight, top_seven],
        [noise_wide.reshape(replicas, rows_eight, padded), noise_seven.reshape(replicas, rows_seven, width)],
        [None, group_seven],
        [0, 0],
        False,
        beside,
        (delta_seven, crossing, [], None),
    )
    grad_six, limit_six, small = small_sums(carried)
    top_six = small[-1]
    (reduced_six,), (reduced_seven, reduced_eight) = scatter(
        [grad_six.reshape(replicas, rows_six, width)],
        [limit_six],
        [top_six],
        [noise_six.reshape(replicas, rows_six, width)],
        [group_six],
        [near_six],
        False,
        [same] * rings + [lambda carried: (carried[0], carried[1].T)],
        (reduced_seven, reduced_eight[:, :outs]),
    )
    grad_pair = small[: 2 * width].reshape(2, width)
    grad_out = small[2 * width : 2 * width + outs]
    squares = (
        jnp.sum(reduced_six * reduced_six)
        + jnp.sum(reduced_seven * reduced_seven)
        + jnp.sum(reduced_eight * reduced_eight)
        + jnp.sum(grad_pair * grad_pair) / replicas
        + jnp.sum(grad_out * grad_out) / (replicas * ways)
    )
    totals = fold(jnp.stack([squares, loss_part]), jnp.add, ("dp", "mp"))
    total_squares, loss = totals[0], totals[1]
    grad_norm = jnp.sqrt(total_squares)
    factor = clip_norm / jnp.maximum(grad_norm, clip_norm)
    new_six, new_m_six, new_v_six = adam_step(
        w_six, m_six, v_six, factor * reduced_six, decay_rate, learn_rate
    )
    new_seven, new_m_seven, new_v_seven = adam_step(
        w_seven, m_seven, v_seven, factor * reduced_seven, decay_rate, learn_rate
    )
    new_eight, new_m_eight, new_v_eight = (
        item.T
        for item in adam_step(
            w_eight.T, m_eight.T, v_eight.T, factor * reduced_eight, decay_rate, learn_rate
        )
    )
    new_biases, new_m_biases, new_v_biases = adam_step(
        biases, m_biases, v_biases, factor * grad_pair, 0.0, bias_rate
    )
    new_bias_out, new_m_bias_out, new_v_bias_out = adam_step(
        bias_out, m_bias_out, v_bias_out, factor * grad_out, 0.0, bias_rate
    )
    return (
        loss,
        grad_norm,
        new_six,
        new_seven,
        new_eight,
        new_m_six,
        new_m_seven,
        new_m_eight,
        new_v_six,
        new_v_seven,
        new_v_eight,
        new_six.astype(jnp.bfloat16),
        new_seven.astype(jnp.bfloat16),
        new_eight.astype(jnp.bfloat16),
        new_biases,
        new_bias_out,
        new_m_biases,
        new_v_biases,
        new_m_bias_out,
        new_v_bias_out,
    )


def solution(mesh):
    return jax.shard_map(
        shards,
        mesh=mesh,
        in_specs=(
            P("dp", "mp"),
            P("dp"),
            P("dp", "mp"),
            P("dp", "mp"),
            P(("dp", "mp"), None),
            P("dp", "mp"),
            P("dp", "mp"),
            P(("mp", "dp"), None),
            P("dp", "mp"),
            P("dp", "mp"),
            P(("mp", "dp"), None),
            P("dp", "mp"),
            P("dp", "mp"),
            P(("mp", "dp"), None),
            P(None, "mp"),
            P(),
            P(None, "mp"),
            P(None, "mp"),
            P(),
            P(),
        ),
        out_specs=(
            P(),
            P(),
            P("dp", "mp"),
            P("dp", "mp"),
            P(("mp", "dp"), None),
            P("dp", "mp"),
            P("dp", "mp"),
            P(("mp", "dp"), None),
            P("dp", "mp"),
            P("dp", "mp"),
            P(("mp", "dp"), None),
            P("dp", "mp"),
            P("dp", "mp"),
            P(("mp", "dp"), None),
            P(None, "mp"),
            P(),
            P(None, "mp"),
            P(None, "mp"),
            P(),
            P(),
        ),
        check_vma=False,
    )
```

```python
import jax
import jax.numpy as jnp
from jax import lax
from jax.sharding import PartitionSpec as P

STEP = 3


beta_one = 0.5
beta_two = 0.5
learn_rate = 0.01
bias_rate = 0.05
decay_rate = 0.1
adam_eps = 1e-08
clip_norm = 0.05
tiny_eps = 1e-12


def matmul(left, right):
    return jnp.dot(left, right, preferred_element_type=jnp.float32)


def contract_rows(left, right):
    return lax.dot_general(
        left, right, (((0,), (0,)), ((), ())), preferred_element_type=jnp.float32
    )


def against_rows(left, right):
    return lax.dot_general(
        left, right, (((1,), (1,)), ((), ())), preferred_element_type=jnp.float32
    )


def layer_forward(pre_sum, bias_row):
    pre_act = pre_sum + bias_row
    return (pre_act, jax.nn.silu(pre_act).astype(jnp.bfloat16))


def layer_delta(pre_act, upstream):
    sigmoid_val = jax.nn.sigmoid(pre_act)
    slope = sigmoid_val * (1.0 + pre_act * (1.0 - sigmoid_val))
    return (upstream * slope).astype(jnp.bfloat16)


def grad_limits(grad_block, columns):
    squares = jnp.sum(grad_block * grad_block)
    limit = 2.5 * jnp.sqrt(squares / (grad_block.shape[0] * columns))
    return (limit, jnp.minimum(jnp.max(jnp.abs(grad_block)), limit))


def swap(value, axis, bit):
    size = lax.axis_size(axis)
    return lax.ppermute(value, axis, [(i, i ^ bit) for i in range(size)])


def turn(value):
    size = lax.axis_size("dp")
    return lax.ppermute(value, "dp", [(i, (i + 2) % size) for i in range(size)])


def spread_bits(axis):
    bit = 1
    while bit < lax.axis_size(axis):
        yield bit
        bit *= 2


def fold(value, combine, axes):
    for axis in axes:
        for bit in spread_bits(axis):
            value = combine(value, swap(value, axis, bit))
    return value


def settle(*values):
    return lax.optimization_barrier(values)


def owner(step, flip):
    size = lax.axis_size("dp")
    here = lax.axis_index("dp")
    return ((here + size - 2 * step) % size) ^ flip


def place(index, blocks):
    if blocks is None:
        return index
    mine = lax.axis_index("mp")
    return ((index // blocks) ^ mine) * blocks + index % blocks


def put(whole, piece, index, row=0):
    return lax.dynamic_update_slice(whole, piece[None], (index, row, 0))


def take(whole, index, row, rows):
    return lax.dynamic_slice(whole, (index, row, 0), (1, rows, whole.shape[2]))[0]


def xor_blocks(value, bits):
    blocks = {0: value}
    for bit in bits:
        blocks |= {step ^ bit: swap(item, "mp", bit) for step, item in blocks.items()}
    return blocks


def near_rows(rows, rings):
    return max(16, (rows // (2 * rings + 2) + 8) // 16 * 16)


def reorder(whole, group):
    if group is None:
        return whole
    mine = lax.axis_index("mp")
    ways = whole.shape[0] // group
    grouped = whole.reshape(ways, group, *whole.shape[1:])
    return jnp.concatenate(
        [lax.dynamic_index_in_dim(grouped, mine ^ step, 0, keepdims=False) for step in range(ways)]
    )


def overlaps(sizes, row, count):
    start = 0
    for spot, size in enumerate(sizes):
        low, high = max(row, start), min(row + count, start + size)
        if low < high:
            yield spot, low - start, high - low, low - row
        start += size


def soft_ternary(grad_block, limit, peak_val, noise_val):
    clipped = jnp.clip(grad_block, -limit, limit)
    ratio = clipped / (peak_val + tiny_eps)
    value = jnp.clip(4.0 * ratio, -1.0, 1.0) * jnp.clip(
        2.0 * (jnp.abs(ratio) - noise_val.astype(jnp.float32)) + 0.5, 0.0, 1.0
    )
    return value.astype(jnp.bfloat16)


def adam_step(weight, moment, second, grad_val, decay, rate):
    moment_new = beta_one * moment + (1.0 - beta_one) * grad_val
    second_new = beta_two * second + (1.0 - beta_two) * grad_val * grad_val
    first_fix = 1.0 - beta_one**STEP
    second_fix = 1.0 - beta_two**STEP
    weight_new = weight - rate * (
        moment_new / first_fix / (jnp.sqrt(second_new / second_fix) + adam_eps) + decay * weight
    )
    return (weight_new, moment_new, second_new)


LONG_RING = 8


def spans_of(rows, count):
    marks = [rows * i // count // 16 * 16 for i in range(count)] + [rows]
    return list(zip(marks[:-1], marks[1:]))


def same(carried):
    return carried


def gather_whole(shard, group):
    return reorder(lax.all_gather(shard, "dp", axis=0), group)


def gather_queue(first, second, groups, near, hooks, carried):
    rings = lax.axis_size("dp") // 2
    rows = first.shape[0]
    middle = rows // 32 * 16
    sizes = [shard.shape[0] for shard in second]
    joined = jnp.concatenate(second)
    cut = joined.shape[0] - near
    ready = {
        ("a", 0): first[:middle],
        ("b", 0): first[middle:],
        ("f", 0): joined[:cut],
        ("n",): joined[cut:],
    }
    z_tasks = [(name, hop) for hop in range(rings - 1) for name in "ab"]
    z_tasks += [(name, hop) for hop in range(rings - 1) for name in "fp"]
    y_tasks = [(name, hop) for hop in range(rings) for name in "ab"]
    y_tasks += [("f", hop) for hop in range(rings)]

    def store(wholes, piece, step, flip, row):
        wholes = list(wholes)
        for spot, inner, count, outer in overlaps(sizes, row, piece.shape[0]):
            index = place(owner(step, flip), groups[1][spot])
            wholes[1 + spot] = put(wholes[1 + spot], piece[outer : outer + count], index, inner)
        return wholes

    def store_first(wholes, piece, step, flip, row):
        index = place(owner(step, flip), groups[0])
        return [put(wholes[0], piece, index, row)] + list(wholes[1:])

    wholes = None
    flight, pending, last = {}, None, {}
    step = 0
    while z_tasks or y_tasks or flight:
        started = {}
        if z_tasks and z_tasks[0] in ready:
            name, hop = z_tasks.pop(0)
            started["z", name, hop + 1] = turn(ready[name, hop])
        if y_tasks and y_tasks[0] in ready:
            name, hop = y_tasks.pop(0)
            started["y", name, hop] = swap(ready[name, hop], "dp", 1)
            if (name, hop) == ("b", rings - 2):
                started["y", "n", 0] = swap(ready["n",], "dp", 1)
        if step == 1:
            wholes = [jnp.zeros((2 * rings, *item.shape), item.dtype) for item in (first, *second)]
            wholes = store_first(wholes, ready["a", 0], 0, 0, 0)
            wholes = store_first(wholes, ready["b", 0], 0, 0, middle)
        if step == 2:
            wholes = store(wholes, ready["f", 0], 0, 0, 0)
            wholes = store(wholes, ready["n",], 0, 0, cut)
        later = None
        if step in hooks:
            carried, later = hooks[step](carried, wholes, last)
        flight, ready, wholes, carried, pending, last = settle(
            flight, ready, wholes, carried, pending, last
        )
        if pending is not None:
            carried = carried | pending
        pending = later
        for (axis, name, hop), piece in flight.items():
            if name in "ab":
                row = 0 if name == "a" else middle
                if axis == "y" and hop == rings - 1:
                    last[name] = piece
                else:
                    wholes = store_first(wholes, piece, hop, int(axis == "y"), row)
            elif name == "f":
                wholes = store(wholes, piece, hop, int(axis == "y"), 0)
            elif name == "n":
                wholes = store(wholes, piece, 0, 1, cut)
                ready["p", 0] = jnp.concatenate([ready["n",], piece])
            else:
                for flip in (0, 1):
                    wholes = store(wholes, piece[flip * near : (flip + 1) * near], hop, flip, cut)
            if axis == "z":
                ready[name, hop] = piece
        flight = started
        step += 1
    return wholes, carried | (pending or {})


def scatter(grads, limits, tops, noises, groups, nears, ahead, beside, carried):
    rings = lax.axis_size("dp") // 2
    if rings > LONG_RING:
        for work in beside:
            carried = work(carried)
        results = []
        for grad, limit, top, noise, group in zip(grads, limits, tops, noises, groups):
            tern = soft_ternary(reorder(grad, group), limit, top, noise)
            total = lax.psum_scatter(tern.astype(jnp.float32), "dp", scatter_dimension=0)
            results.append(top * total)
        return results, carried
    beside = beside + [same] * (2 * rings - len(beside))
    spots = range(len(grads))
    cuts = [grad.shape[1] - near for grad, near in zip(grads, nears)]
    hops = rings - 1 if any(nears) else 1
    cutting = [
        spans_of(cut, hops) if near else [(0, cut)] + [None] * (hops - 1)
        for cut, near in zip(cuts, nears)
    ]

    ready = [
        soft_ternary(grad, limit, top, noise) if group is None else None
        for grad, limit, top, noise, group in zip(grads, limits, tops, noises, groups)
    ]

    def tern(spot, step, flip, row, count):
        index = owner(step, flip)
        if ready[spot] is not None:
            return take(ready[spot], index, row, count)
        return soft_ternary(
            take(grads[spot], place(index, groups[spot]), row, count),
            limits[spot],
            tops[spot],
            take(noises[spot], index, row, count),
        )

    def terns(step, flip, spans):
        return [
            None if span is None else tern(spot, step, flip, span[0], span[1] - span[0])
            for spot, span in zip(spots, spans)
        ]

    def far_terns(step, flip):
        return terns(step, flip, [(0, cut) for cut in cuts])

    def near_terns(step):
        return [
            jnp.concatenate([tern(spot, step, flip, cuts[spot], nears[spot]) for flip in (0, 1)])
            if nears[spot]
            else None
            for spot in spots
        ]

    def each(work, *lists):
        return [None if items[0] is None else work(*items) for items in zip(*lists)]

    def wide(value):
        return value.astype(jnp.float32)

    def narrow(value):
        return value.astype(jnp.bfloat16)

    def across(value):
        return swap(value, "dp", 1)

    order = list(range(1, rings)) + [0]
    pairs = near_terns(order[0])
    sending = [terns(order[0], 1, [cut[0] for cut in cutting])]
    pairs, sending, limits, carried, ready = settle(pairs, sending, limits, carried, ready)
    aways, owns = {}, {}
    got = [[] for spot in spots]
    for hop in range(1, hops + 1):
        others = each(across, sending[hop - 1])
        arrived = each(lambda item: turn(narrow(item)), pairs)
        more = near_terns(order[hop])
        if hop < hops:
            sending.append(terns(order[0], 1, [cut[hop] for cut in cutting]))
        if hop == 1:
            owns[0] = far_terns(order[0], 0)
        if hop == hops:
            aways[1] = far_terns(order[1], 1)
        carried = beside[hop - 1](carried)
        others, arrived, more, sending, aways, owns, limits, carried = settle(
            others, arrived, more, sending, aways, owns, limits, carried
        )
        pairs = each(lambda item, add: wide(item) + wide(add), arrived, more)
        for spot in spots:
            if others[spot] is not None:
                got[spot].append(others[spot])
    sums = [wide(owns[0][spot]) + wide(jnp.concatenate(got[spot])) for spot in spots]
    for spin in range(1, rings):
        others = each(across, aways[spin])
        moved = each(lambda item: turn(narrow(item)), sums)
        lasts = None
        if spin == rings - 1:
            lasts = [
                item if item is None else across(narrow(item[near:]))
                for item, near in zip(pairs, nears)
            ]
        for later in range(spin, rings if ahead else spin + 1):
            if later not in owns:
                owns[later] = far_terns(order[later], 0)
        for later in range(spin + 1, rings if ahead else min(spin + 2, rings)):
            if later not in aways:
                aways[later] = far_terns(order[later], 1)
        carried = beside[hops - 1 + spin](carried)
        others, moved, lasts, pairs, aways, owns, limits, carried = settle(
            others, moved, lasts, pairs, aways, owns, limits, carried
        )
        sums = each(
            lambda own, item, more: wide(own) + wide(item) + wide(more), owns[spin], others, moved
        )
    results = []
    for spot, near in zip(spots, nears):
        total = sums[spot]
        if near:
            total = jnp.concatenate([total, pairs[spot][:near] + wide(lasts[spot])])
        results.append(tops[spot] * total)
    return results, carried


def shards(
    features,
    labels,
    noise_six,
    noise_seven,
    noise_eight,
    w_six,
    w_seven,
    w_eight,
    m_six,
    m_seven,
    m_eight,
    v_six,
    v_seven,
    v_eight,
    biases,
    bias_out,
    m_biases,
    v_biases,
    m_bias_out,
    v_bias_out,
):
    mine = lax.axis_index("mp")
    replicas = lax.axis_size("dp")
    ways = lax.axis_size("mp")
    rings = replicas // 2
    batch_rows = features.shape[0]
    tokens = batch_rows * replicas
    half = batch_rows // 2
    width = biases.shape[1]
    outs = bias_out.shape[0]
    padded = outs + -outs % 128
    rows_six, rows_seven, rows_eight = w_six.shape[0], w_seven.shape[0], w_eight.shape[0]
    group_six, group_seven = features.shape[1] // rows_six, width // rows_seven
    near_six = near_rows(rows_six, rings)
    bits = list(reversed(list(spread_bits("mp"))))
    far_bits, near_bit = bits[:-1], bits[-1]

    def widen(value):
        return jnp.pad(value, ((0, 0), (0, padded - outs)))

    def halves(value):
        return [value[:half], value[half:]]

    def over_far(own):
        done = xor_blocks(own, far_bits)
        del done[0]
        return done

    def over_near(blocks):
        return {step ^ near_bit: swap(item, "mp", near_bit) for step, item in blocks.items()}

    def join(halves_of_blocks):
        return jnp.concatenate(
            [
                jnp.concatenate([blocks[step] for step in range(ways)], axis=1)
                for blocks in halves_of_blocks
            ]
        )

    far_features = over_far(features)
    shards_cast = [
        w_six.astype(jnp.bfloat16),
        widen(w_eight.astype(jnp.bfloat16)),
        w_seven.astype(jnp.bfloat16),
    ]
    if rings > LONG_RING:
        inputs = join([{0: features} | far_features | over_near({0: features} | far_features)])
        noise_wide = widen(noise_eight)
        kept_six = gather_whole(shards_cast[0], group_six).reshape(-1, width)
        kept_eight = gather_whole(shards_cast[1], None)
        kept_seven = gather_whole(shards_cast[2], group_seven)
        pre_six, out_six = layer_forward(matmul(inputs, kept_six), biases[0])
        hidden_blocks = []
        for item in halves(out_six):
            blocks = {0: item} | over_far(item)
            hidden_blocks.append(blocks | over_near(blocks))
    else:
        count = 2 * rings

        def own_near(carried, wholes, last):
            return {"near": swap(features, "mp", near_bit), "noise": widen(noise_eight)}, None

        def far_there(carried, wholes, last):
            return carried | {"far": far_features}, None

        def far_near(carried, wholes, last):
            return carried | {"both": over_near(carried["far"])}, None

        def join_inputs(carried, wholes, last):
            blocks = {0: features, near_bit: carried["near"]} | carried["far"] | carried["both"]
            return {"inputs": join([blocks]), "noise": carried["noise"]}, None

        def fc_six_most(carried, wholes, last):
            early = matmul(carried["inputs"], wholes[0].reshape(-1, width))
            return carried, {"early": early}

        def fc_six_rest(carried, wholes, last):
            start = place(owner(rings - 1, 1), group_six) * rows_six
            columns = lax.dynamic_slice_in_dim(carried["inputs"], start, rows_six, 1)
            rest = matmul(columns, jnp.concatenate([last["a"], last["b"]]))
            pre_six, out_six = layer_forward(carried["early"] + rest, biases[0])
            one, two = halves(out_six)
            crossing["one"], crossing["two"] = over_far(one), over_far(two)
            return (
                {"inputs": carried["inputs"], "noise": carried["noise"], "pre": pre_six, "out": (one, two)},
                None,
            )

        crossing = {}

        def hidden_own(carried, wholes, last):
            own = [over_near({0: item}) for item in carried["out"]]
            return carried | {"own": own}, None

        def hidden_one(carried, wholes, last):
            return carried | {"one": crossing["one"]}, None

        def hidden_one_near(carried, wholes, last):
            return carried | {"one_near": over_near(carried["one"])}, None

        hooks = {
            1: own_near,
            count - 4: far_there,
            count - 3: far_near,
            count - 2: join_inputs,
            count - 1: fc_six_most,
            count + 1: fc_six_rest,
            count + 2: hidden_own,
            count + 3: hidden_one,
            count + 4: hidden_one_near,
        }
        near = (rows_six + rows_seven + rows_eight) // (2 * rings - 2) // 16 * 16
        (_, kept_eight, kept_seven), carried = gather_queue(
            shards_cast[0],
            shards_cast[1:],
            [group_six, [None, group_seven]],
            min(near, rows_seven // 32 * 16),
            hooks,
            {},
        )
        inputs, noise_wide, pre_six = carried["inputs"], carried["noise"], carried["pre"]
        one, two = carried["out"]
        hidden_blocks = [
            {0: one} | carried["own"][0] | carried["one"] | carried["one_near"],
            {0: two} | carried["own"][1] | crossing["two"] | over_near(crossing["two"]),
        ]
    kept_seven, kept_eight = kept_seven.reshape(-1, width), kept_eight.reshape(-1, padded)

    bias_wide = jnp.pad(bias_out, (0, padded - outs), constant_values=-1e30)
    share = half // ways

    def half_forward(number):
        pre, out = layer_forward(matmul(join([hidden_blocks[number]]), kept_seven), biases[1])
        shares = out.reshape(ways, share, width)
        parts = {
            step: matmul(lax.dynamic_index_in_dim(shares, mine ^ step, 0, keepdims=False), kept_eight)
            for step in range(ways)
        }
        for bit in reversed(bits):
            for step in range(0, ways, 2 * bit):
                parts[step] = parts[step] + swap(parts[step + bit], "mp", bit)
        logits = parts[0] + bias_wide
        labels_part = lax.dynamic_slice_in_dim(labels, number * half + mine * share, share, 0)
        top_logit = jnp.max(logits, axis=1, keepdims=True)
        shifted = jnp.exp(logits - top_logit)
        row_total = jnp.sum(shifted, axis=1, keepdims=True)
        log_total = top_logit[:, 0] + jnp.log(row_total[:, 0])
        classes = lax.broadcasted_iota(jnp.int32, logits.shape, 1)
        onehot = (classes == labels_part[:, None]).astype(jnp.float32)
        loss_part = jnp.sum(log_total - jnp.sum(onehot * logits, axis=1)) / tokens
        dz_part = ((shifted / row_total - onehot) / tokens).astype(jnp.bfloat16)
        dlogits = jnp.zeros((ways, share, padded), jnp.bfloat16)
        for step, item in xor_blocks(dz_part, bits).items():
            dlogits = put(dlogits, item, mine ^ step)
        return pre, out, dlogits.reshape(half, padded), loss_part

    both = [half_forward(number) for number in (0, 1)]
    pre_seven, out_seven, dlogits = (
        jnp.concatenate([item[spot] for item in both]) for spot in range(3)
    )
    loss_part = both[0][3] + both[1][3]
    hidden = join(hidden_blocks)

    delta_seven = layer_delta(pre_seven, against_rows(dlogits, kept_eight))

    def upstream(delta, step):
        return against_rows(delta, kept_seven[step * width : (step + 1) * width])

    top_bit = bits[0]
    cuts = [0, batch_rows // 64 * 22, batch_rows // 64 * 43, batch_rows]

    def near_sums(first, delta):
        ups = {step: upstream(delta, step) for step in range(first, first + top_bit)}
        for bit in reversed(bits[1:]):
            for step in range(first, first + top_bit, 2 * bit):
                ups[step] = ups[step] + swap(ups[step + bit], "mp", bit)
        return ups[first]

    crossing = near_sums(top_bit, delta_seven)
    grad_eight = contract_rows(out_seven, dlogits)
    limit_eight, peak_eight = grad_limits(grad_eight, outs)
    crossing, grad_eight, limit_eight, peak_eight, delta_seven, dlogits = settle(
        crossing, grad_eight, limit_eight, peak_eight, delta_seven, dlogits
    )
    crossing = [crossing[low:high] for low, high in zip(cuts[:-1], cuts[1:])]
    grad_seven = contract_rows(hidden, delta_seven)
    limit_seven, peak_seven = grad_limits(grad_seven, width)
    tops = fold(jnp.stack([peak_eight, peak_seven]), jnp.maximum, ("dp",))
    crossing, grad_seven, limit_seven, tops, delta_seven = settle(
        crossing, grad_seven, limit_seven, tops, delta_seven
    )
    top_eight, top_seven = tops[0], tops[1]

    def cross(step):
        def work(carried):
            delta, crossing, crossed, own_up = carried
            if step == 0:
                own_up = near_sums(0, delta)
            return (delta, crossing, crossed + [swap(crossing[step], "mp", top_bit)], own_up)

        return work

    def grad_fc_six(carried):
        _, _, crossed, own_up = carried
        delta_six = layer_delta(pre_six, own_up + jnp.concatenate(crossed))
        grad_six = contract_rows(inputs, delta_six)
        limit_six, peak_six = grad_limits(grad_six, width)
        return (delta_six, grad_six, limit_six, peak_six)

    def sum_or_max(one, two):
        return jnp.concatenate([one[:-1] + two[:-1], jnp.maximum(one[-1:], two[-1:])])

    def small_sums(carried):
        delta_six, grad_six, limit_six, peak_six = carried
        columns = [
            jnp.sum(item.astype(jnp.float32), axis=0) for item in (delta_six, delta_seven, dlogits)
        ]
        small = fold(jnp.concatenate(columns + [peak_six[None]]), sum_or_max, ("dp",))
        return (grad_six, limit_six, small)

    beside = [
        cross(0),
        cross(1),
        cross(2),
        grad_fc_six,
    ]
    (reduced_eight, reduced_seven), carried = scatter(
        [grad_eight.reshape(replicas, rows_eight, padded), grad_seven.reshape(replicas, rows_seven, width)],
        [limit_eight, limit_seven],
        [top_eight, top_seven],
        [noise_wide.reshape(replicas, rows_eight, padded), noise_seven.reshape(replicas, rows_seven, width)],
        [None, group_seven],
        [0, 0],
        False,
        beside,
        (delta_seven, crossing, [], None),
    )
    grad_six, limit_six, small = small_sums(carried)
    top_six = small[-1]
    (reduced_six,), (reduced_seven, reduced_eight) = scatter(
        [grad_six.reshape(replicas, rows_six, width)],
        [limit_six],
        [top_six],
        [noise_six.reshape(replicas, rows_six, width)],
        [group_six],
        [near_six],
        False,
        [same] * rings + [lambda carried: (carried[0], carried[1].T)],
        (reduced_seven, reduced_eight[:, :outs]),
    )
    grad_pair = small[: 2 * width].reshape(2, width)
    grad_out = small[2 * width : 2 * width + outs]
    squares = (
        jnp.sum(reduced_six * reduced_six)
        + jnp.sum(reduced_seven * reduced_seven)
        + jnp.sum(reduced_eight * reduced_eight)
        + jnp.sum(grad_pair * grad_pair) / replicas
        + jnp.sum(grad_out * grad_out) / (replicas * ways)
    )
    totals = fold(jnp.stack([squares, loss_part]), jnp.add, ("dp", "mp"))
    total_squares, loss = totals[0], totals[1]
    grad_norm = jnp.sqrt(total_squares)
    factor = clip_norm / jnp.maximum(grad_norm, clip_norm)
    new_six, new_m_six, new_v_six = adam_step(
        w_six, m_six, v_six, factor * reduced_six, decay_rate, learn_rate
    )
    new_seven, new_m_seven, new_v_seven = adam_step(
        w_seven, m_seven, v_seven, factor * reduced_seven, decay_rate, learn_rate
    )
    new_eight, new_m_eight, new_v_eight = (
        item.T
        for item in adam_step(
            w_eight.T, m_eight.T, v_eight.T, factor * reduced_eight, decay_rate, learn_rate
        )
    )
    new_biases, new_m_biases, new_v_biases = adam_step(
        biases, m_biases, v_biases, factor * grad_pair, 0.0, bias_rate
    )
    new_bias_out, new_m_bias_out, new_v_bias_out = adam_step(
        bias_out, m_bias_out, v_bias_out, factor * grad_out, 0.0, bias_rate
    )
    return (
        loss,
        grad_norm,
        new_six,
        new_seven,
        new_eight,
        new_m_six,
        new_m_seven,
        new_m_eight,
        new_v_six,
        new_v_seven,
        new_v_eight,
        new_six.astype(jnp.bfloat16),
        new_seven.astype(jnp.bfloat16),
        new_eight.astype(jnp.bfloat16),
        new_biases,
        new_bias_out,
        new_m_biases,
        new_v_biases,
        new_m_bias_out,
        new_v_bias_out,
    )


def solution(mesh):
    return jax.shard_map(
        shards,
        mesh=mesh,
        in_specs=(
            P("dp", "mp"),
            P("dp"),
            P("dp", "mp"),
            P("dp", "mp"),
            P(("dp", "mp"), None),
            P("dp", "mp"),
            P("dp", "mp"),
            P(("mp", "dp"), None),
            P("dp", "mp"),
            P("dp", "mp"),
            P(("mp", "dp"), None),
            P("dp", "mp"),
            P("dp", "mp"),
            P(("mp", "dp"), None),
            P(None, "mp"),
            P(),
            P(None, "mp"),
            P(None, "mp"),
            P(),
            P(),
        ),
        out_specs=(
            P(),
            P(),
            P("dp", "mp"),
            P("dp", "mp"),
            P(("mp", "dp"), None),
            P("dp", "mp"),
            P("dp", "mp"),
            P(("mp", "dp"), None),
            P("dp", "mp"),
            P("dp", "mp"),
            P(("mp", "dp"), None),
            P("dp", "mp"),
            P("dp", "mp"),
            P(("mp", "dp"), None),
            P(None, "mp"),
            P(),
            P(None, "mp"),
            P(None, "mp"),
            P(),
            P(),
        ),
        check_vma=False,
    )
```

```python
import jax
import jax.numpy as jnp
from jax import lax
from jax.sharding import PartitionSpec as P

STEP = 3


beta_one = 0.5
beta_two = 0.5
learn_rate = 0.01
bias_rate = 0.05
decay_rate = 0.1
adam_eps = 1e-08
clip_norm = 0.05
tiny_eps = 1e-12


def matmul(left, right):
    return jnp.dot(left, right, preferred_element_type=jnp.float32)


def contract_rows(left, right):
    return lax.dot_general(
        left, right, (((0,), (0,)), ((), ())), preferred_element_type=jnp.float32
    )


def against_rows(left, right):
    return lax.dot_general(
        left, right, (((1,), (1,)), ((), ())), preferred_element_type=jnp.float32
    )


def layer_forward(pre_sum, bias_row):
    pre_act = pre_sum + bias_row
    return (pre_act, jax.nn.silu(pre_act).astype(jnp.bfloat16))


def layer_delta(pre_act, upstream):
    sigmoid_val = jax.nn.sigmoid(pre_act)
    slope = sigmoid_val * (1.0 + pre_act * (1.0 - sigmoid_val))
    return (upstream * slope).astype(jnp.bfloat16)


def grad_limits(grad_block, columns):
    squares = jnp.sum(grad_block * grad_block)
    limit = 2.5 * jnp.sqrt(squares / (grad_block.shape[0] * columns))
    return (limit, jnp.minimum(jnp.max(jnp.abs(grad_block)), limit))


def swap(value, axis, bit):
    size = lax.axis_size(axis)
    return lax.ppermute(value, axis, [(i, i ^ bit) for i in range(size)])


def turn(value):
    size = lax.axis_size("dp")
    return lax.ppermute(value, "dp", [(i, (i + 2) % size) for i in range(size)])


def spread_bits(axis):
    bit = 1
    while bit < lax.axis_size(axis):
        yield bit
        bit *= 2


def fold(value, combine, axes):
    for axis in axes:
        for bit in spread_bits(axis):
            value = combine(value, swap(value, axis, bit))
    return value


def settle(*values):
    return lax.optimization_barrier(values)


def owner(step, flip):
    size = lax.axis_size("dp")
    here = lax.axis_index("dp")
    return ((here + size - 2 * step) % size) ^ flip


def place(index, blocks):
    if blocks is None:
        return index
    mine = lax.axis_index("mp")
    return ((index // blocks) ^ mine) * blocks + index % blocks


def put(whole, piece, index, row=0):
    return lax.dynamic_update_slice(whole, piece[None], (index, row, 0))


def take(whole, index, row, rows):
    return lax.dynamic_slice(whole, (index, row, 0), (1, rows, whole.shape[2]))[0]


def xor_blocks(value, bits):
    blocks = {0: value}
    for bit in bits:
        blocks |= {step ^ bit: swap(item, "mp", bit) for step, item in blocks.items()}
    return blocks


def near_rows(rows, rings):
    return max(16, (rows // (2 * rings + 2) + 8) // 16 * 16)


def reorder(whole, group):
    if group is None:
        return whole
    mine = lax.axis_index("mp")
    ways = whole.shape[0] // group
    grouped = whole.reshape(ways, group, *whole.shape[1:])
    return jnp.concatenate(
        [lax.dynamic_index_in_dim(grouped, mine ^ step, 0, keepdims=False) for step in range(ways)]
    )


def overlaps(sizes, row, count):
    start = 0
    for spot, size in enumerate(sizes):
        low, high = max(row, start), min(row + count, start + size)
        if low < high:
            yield spot, low - start, high - low, low - row
        start += size


def soft_ternary(grad_block, limit, peak_val, noise_val):
    clipped = jnp.clip(grad_block, -limit, limit)
    ratio = clipped / (peak_val + tiny_eps)
    value = jnp.clip(4.0 * ratio, -1.0, 1.0) * jnp.clip(
        2.0 * (jnp.abs(ratio) - noise_val.astype(jnp.float32)) + 0.5, 0.0, 1.0
    )
    return value.astype(jnp.bfloat16)


def adam_step(weight, moment, second, grad_val, decay, rate):
    moment_new = beta_one * moment + (1.0 - beta_one) * grad_val
    second_new = beta_two * second + (1.0 - beta_two) * grad_val * grad_val
    first_fix = 1.0 - beta_one**STEP
    second_fix = 1.0 - beta_two**STEP
    weight_new = weight - rate * (
        moment_new / first_fix / (jnp.sqrt(second_new / second_fix) + adam_eps) + decay * weight
    )
    return (weight_new, moment_new, second_new)


LONG_RING = 8


def spans_of(rows, count):
    marks = [rows * i // count // 16 * 16 for i in range(count)] + [rows]
    return list(zip(marks[:-1], marks[1:]))


def same(carried):
    return carried


def gather_whole(shard, group):
    return reorder(lax.all_gather(shard, "dp", axis=0), group)


def gather_queue(first, second, groups, near, hooks, carried):
    rings = lax.axis_size("dp") // 2
    rows = first.shape[0]
    middle = rows // 32 * 16
    sizes = [shard.shape[0] for shard in second]
    joined = jnp.concatenate(second)
    cut = joined.shape[0] - near
    ready = {
        ("a", 0): first[:middle],
        ("b", 0): first[middle:],
        ("f", 0): joined[:cut],
        ("n",): joined[cut:],
    }
    z_tasks = [(name, hop) for hop in range(rings - 1) for name in "ab"]
    z_tasks += [(name, hop) for hop in range(rings - 1) for name in "fp"]
    y_tasks = [(name, hop) for hop in range(rings) for name in "ab"]
    y_tasks += [("f", hop) for hop in range(rings)]

    def store(wholes, piece, step, flip, row):
        wholes = list(wholes)
        for spot, inner, count, outer in overlaps(sizes, row, piece.shape[0]):
            index = place(owner(step, flip), groups[1][spot])
            wholes[1 + spot] = put(wholes[1 + spot], piece[outer : outer + count], index, inner)
        return wholes

    def store_first(wholes, piece, step, flip, row):
        index = place(owner(step, flip), groups[0])
        return [put(wholes[0], piece, index, row)] + list(wholes[1:])

    wholes = None
    flight, pending, last = {}, None, {}
    step = 0
    while z_tasks or y_tasks or flight:
        started = {}
        if z_tasks and z_tasks[0] in ready:
            name, hop = z_tasks.pop(0)
            started["z", name, hop + 1] = turn(ready[name, hop])
        if y_tasks and y_tasks[0] in ready:
            name, hop = y_tasks.pop(0)
            started["y", name, hop] = swap(ready[name, hop], "dp", 1)
            if (name, hop) == ("b", rings - 2):
                started["y", "n", 0] = swap(ready["n",], "dp", 1)
        if step == 1:
            wholes = [jnp.zeros((2 * rings, *item.shape), item.dtype) for item in (first, *second)]
            wholes = store_first(wholes, ready["a", 0], 0, 0, 0)
            wholes = store_first(wholes, ready["b", 0], 0, 0, middle)
        if step == 2:
            wholes = store(wholes, ready["f", 0], 0, 0, 0)
            wholes = store(wholes, ready["n",], 0, 0, cut)
        later = None
        if step in hooks:
            carried, later = hooks[step](carried, wholes, last)
        flight, ready, wholes, carried, pending, last = settle(
            flight, ready, wholes, carried, pending, last
        )
        if pending is not None:
            carried = carried | pending
        pending = later
        for (axis, name, hop), piece in flight.items():
            if name in "ab":
                row = 0 if name == "a" else middle
                if axis == "y" and hop == rings - 1:
                    last[name] = piece
                else:
                    wholes = store_first(wholes, piece, hop, int(axis == "y"), row)
            elif name == "f":
                wholes = store(wholes, piece, hop, int(axis == "y"), 0)
                if axis == "y" and hop == rings - 1:
                    last[name] = piece
            elif name == "n":
                wholes = store(wholes, piece, 0, 1, cut)
                ready["p", 0] = jnp.concatenate([ready["n",], piece])
            else:
                if hop == rings - 1:
                    last[name] = piece
                for flip in (0, 1):
                    wholes = store(wholes, piece[flip * near : (flip + 1) * near], hop, flip, cut)
            if axis == "z":
                ready[name, hop] = piece
        flight = started
        step += 1
    return wholes, last, carried | (pending or {})


def scatter(grads, limits, tops, noises, groups, nears, ahead, beside, carried):
    rings = lax.axis_size("dp") // 2
    if rings > LONG_RING:
        for work in beside:
            carried = work(carried)
        results = []
        for grad, limit, top, noise, group in zip(grads, limits, tops, noises, groups):
            tern = soft_ternary(reorder(grad, group), limit, top, noise)
            total = lax.psum_scatter(tern.astype(jnp.float32), "dp", scatter_dimension=0)
            results.append(top * total)
        return results, carried
    beside = beside + [same] * (2 * rings - len(beside))
    spots = range(len(grads))
    cuts = [grad.shape[1] - near for grad, near in zip(grads, nears)]
    hops = rings - 1 if any(nears) else 1
    cutting = [
        spans_of(cut, hops) if near else [(0, cut)] + [None] * (hops - 1)
        for cut, near in zip(cuts, nears)
    ]

    ready = [
        soft_ternary(grad, limit, top, noise) if group is None else None
        for grad, limit, top, noise, group in zip(grads, limits, tops, noises, groups)
    ]

    def tern(spot, step, flip, row, count):
        index = owner(step, flip)
        if ready[spot] is not None:
            return take(ready[spot], index, row, count)
        return soft_ternary(
            take(grads[spot], place(index, groups[spot]), row, count),
            limits[spot],
            tops[spot],
            take(noises[spot], index, row, count),
        )

    def terns(step, flip, spans):
        return [
            None if span is None else tern(spot, step, flip, span[0], span[1] - span[0])
            for spot, span in zip(spots, spans)
        ]

    def far_terns(step, flip):
        return terns(step, flip, [(0, cut) for cut in cuts])

    def near_terns(step):
        return [
            jnp.concatenate([tern(spot, step, flip, cuts[spot], nears[spot]) for flip in (0, 1)])
            if nears[spot]
            else None
            for spot in spots
        ]

    def each(work, *lists):
        return [None if items[0] is None else work(*items) for items in zip(*lists)]

    def wide(value):
        return value.astype(jnp.float32)

    def narrow(value):
        return value.astype(jnp.bfloat16)

    def across(value):
        return swap(value, "dp", 1)

    order = list(range(1, rings)) + [0]
    pairs = near_terns(order[0])
    sending = [terns(order[0], 1, [cut[0] for cut in cutting])]
    pairs, sending, limits, carried, ready = settle(pairs, sending, limits, carried, ready)
    aways, owns = {}, {}
    got = [[] for spot in spots]
    for hop in range(1, hops + 1):
        others = each(across, sending[hop - 1])
        arrived = each(lambda item: turn(narrow(item)), pairs)
        more = near_terns(order[hop])
        if hop < hops:
            sending.append(terns(order[0], 1, [cut[hop] for cut in cutting]))
        if hop == 1:
            owns[0] = far_terns(order[0], 0)
        if hop == hops:
            aways[1] = far_terns(order[1], 1)
        carried = beside[hop - 1](carried)
        others, arrived, more, sending, aways, owns, limits, carried = settle(
            others, arrived, more, sending, aways, owns, limits, carried
        )
        pairs = each(lambda item, add: wide(item) + wide(add), arrived, more)
        for spot in spots:
            if others[spot] is not None:
                got[spot].append(others[spot])
    sums = [wide(owns[0][spot]) + wide(jnp.concatenate(got[spot])) for spot in spots]
    for spin in range(1, rings):
        others = each(across, aways[spin])
        moved = each(lambda item: turn(narrow(item)), sums)
        lasts = None
        if spin == rings - 1:
            lasts = [
                item if item is None else across(narrow(item[near:]))
                for item, near in zip(pairs, nears)
            ]
        for later in range(spin, rings if ahead else spin + 1):
            if later not in owns:
                owns[later] = far_terns(order[later], 0)
        for later in range(spin + 1, rings if ahead else min(spin + 2, rings)):
            if later not in aways:
                aways[later] = far_terns(order[later], 1)
        carried = beside[hops - 1 + spin](carried)
        others, moved, lasts, pairs, aways, owns, limits, carried = settle(
            others, moved, lasts, pairs, aways, owns, limits, carried
        )
        sums = each(
            lambda own, item, more: wide(own) + wide(item) + wide(more), owns[spin], others, moved
        )
    results = []
    for spot, near in zip(spots, nears):
        total = sums[spot]
        if near:
            total = jnp.concatenate([total, pairs[spot][:near] + wide(lasts[spot])])
        results.append(tops[spot] * total)
    return results, carried


def shards(
    features,
    labels,
    noise_six,
    noise_seven,
    noise_eight,
    w_six,
    w_seven,
    w_eight,
    m_six,
    m_seven,
    m_eight,
    v_six,
    v_seven,
    v_eight,
    biases,
    bias_out,
    m_biases,
    v_biases,
    m_bias_out,
    v_bias_out,
):
    mine = lax.axis_index("mp")
    replicas = lax.axis_size("dp")
    ways = lax.axis_size("mp")
    rings = replicas // 2
    batch_rows = features.shape[0]
    tokens = batch_rows * replicas
    half = batch_rows // 2
    width = biases.shape[1]
    outs = bias_out.shape[0]
    padded = outs + -outs % 128
    rows_six, rows_seven, rows_eight = w_six.shape[0], w_seven.shape[0], w_eight.shape[0]
    group_six, group_seven = features.shape[1] // rows_six, width // rows_seven
    near_six = near_rows(rows_six, rings)
    bits = list(reversed(list(spread_bits("mp"))))
    far_bits, near_bit = bits[:-1], bits[-1]

    def widen(value):
        return jnp.pad(value, ((0, 0), (0, padded - outs)))

    def halves(value):
        return [value[:half], value[half:]]

    def over_far(own):
        done = xor_blocks(own, far_bits)
        del done[0]
        return done

    def over_near(blocks):
        return {step ^ near_bit: swap(item, "mp", near_bit) for step, item in blocks.items()}

    def join(halves_of_blocks):
        return jnp.concatenate(
            [
                jnp.concatenate([blocks[step] for step in range(ways)], axis=1)
                for blocks in halves_of_blocks
            ]
        )

    far_features = over_far(features)
    shards_cast = [
        w_six.astype(jnp.bfloat16),
        widen(w_eight.astype(jnp.bfloat16)),
        w_seven.astype(jnp.bfloat16),
    ]
    if rings > LONG_RING:
        inputs = join([{0: features} | far_features | over_near({0: features} | far_features)])
        noise_wide = widen(noise_eight)
        kept_six = gather_whole(shards_cast[0], group_six).reshape(-1, width)
        kept_eight = gather_whole(shards_cast[1], None)
        kept_seven = gather_whole(shards_cast[2], group_seven)
        pre_six, out_six = layer_forward(matmul(inputs, kept_six), biases[0])
        hidden_blocks = []
        for item in halves(out_six):
            blocks = {0: item} | over_far(item)
            hidden_blocks.append(blocks | over_near(blocks))
        hiddens = [join([blocks]) for blocks in hidden_blocks]

        def sum_seven(number):
            return matmul(hiddens[number], kept_seven.reshape(-1, width))

    else:
        count = 2 * rings

        def own_near(carried, wholes, last):
            return {"near": swap(features, "mp", near_bit), "noise": widen(noise_eight)}, None

        def far_there(carried, wholes, last):
            return carried | {"far": far_features}, None

        def far_near(carried, wholes, last):
            return carried | {"both": over_near(carried["far"])}, None

        def join_inputs(carried, wholes, last):
            blocks = {0: features, near_bit: carried["near"]} | carried["far"] | carried["both"]
            return {"inputs": join([blocks]), "noise": carried["noise"]}, None

        def fc_six_most(carried, wholes, last):
            early = matmul(carried["inputs"], wholes[0].reshape(-1, width))
            return carried, {"early": early}

        def fc_six_rest(carried, wholes, last):
            start = place(owner(rings - 1, 1), group_six) * rows_six
            columns = lax.dynamic_slice_in_dim(carried["inputs"], start, rows_six, 1)
            rest = matmul(columns, jnp.concatenate([last["a"], last["b"]]))
            pre_six, out_six = layer_forward(carried["early"] + rest, biases[0])
            one, two = halves(out_six)
            crossing["one"], crossing["two"] = over_far(one), over_far(two)
            return (
                {"inputs": carried["inputs"], "noise": carried["noise"], "pre": pre_six, "out": (one, two)},
                None,
            )

        crossing = {}

        def hidden_own(carried, wholes, last):
            own = [over_near({0: item}) for item in carried["out"]]
            return carried | {"own": own}, None

        def hidden_one(carried, wholes, last):
            return carried | {"one": crossing["one"]}, None

        def hidden_one_near(carried, wholes, last):
            blocks = {0: carried["out"][0]} | carried["own"][0] | carried["one"]
            hidden = join([blocks | over_near(carried["one"])])
            early = matmul(hidden, wholes[2].reshape(-1, width))
            return carried, {"hidden_one": hidden, "early_one": early}

        def fc_seven_most(carried, wholes, last):
            far = crossing["two"]
            two = join([{0: carried["out"][1]} | carried["own"][1] | far | over_near(far)])
            early = matmul(two, wholes[2].reshape(-1, width))
            names = ("inputs", "noise", "pre")
            return {name: carried[name] for name in names} | {"hidden_two": two, "early_two": early}, None

        hooks = {
            1: own_near,
            count - 4: far_there,
            count - 3: far_near,
            count - 2: join_inputs,
            count - 1: fc_six_most,
            count + 1: fc_six_rest,
            count + 2: hidden_own,
            count + 3: hidden_one,
            count + 4: hidden_one_near,
            count + 5: fc_seven_most,
        }
        near = (rows_six + rows_seven + rows_eight) // (2 * rings - 2) // 16 * 16
        (_, kept_eight, kept_seven), last, carried = gather_queue(
            shards_cast[0],
            shards_cast[1:],
            [group_six, [None, group_seven]],
            min(near, rows_seven // 32 * 16),
            hooks,
            {},
        )
        inputs, noise_wide, pre_six = carried["inputs"], carried["noise"], carried["pre"]
        hiddens = [carried["hidden_one"], carried["hidden_two"]]
        start = place(owner(rings - 1, 1), group_seven) * rows_seven
        other_start = place(owner(rings - 1, 0), group_seven) * rows_seven
        rest = last["f"][rows_eight:]
        count, most = last["p"].shape[0] // 2, rest.shape[0]

        def columns(number, low, size):
            return lax.dynamic_slice_in_dim(hiddens[number], low, size, 1)

        def sum_seven(number):
            if number == 1:
                return carried["early_two"] + matmul(columns(1, start, most), rest)
            whole_block = jnp.concatenate([rest, last["p"][count:]])
            return (
                carried["early_one"]
                + matmul(columns(0, start, rows_seven), whole_block)
                + matmul(columns(0, other_start + most, count), last["p"][:count])
            )

    kept_seven, kept_eight = kept_seven.reshape(-1, width), kept_eight.reshape(-1, padded)

    bias_wide = jnp.pad(bias_out, (0, padded - outs), constant_values=-1e30)
    share = half // ways

    def half_forward(number):
        pre, out = layer_forward(sum_seven(number), biases[1])
        shares = out.reshape(ways, share, width)
        parts = {
            step: matmul(lax.dynamic_index_in_dim(shares, mine ^ step, 0, keepdims=False), kept_eight)
            for step in range(ways)
        }
        for bit in reversed(bits):
            for step in range(0, ways, 2 * bit):
                parts[step] = parts[step] + swap(parts[step + bit], "mp", bit)
        logits = parts[0] + bias_wide
        labels_part = lax.dynamic_slice_in_dim(labels, number * half + mine * share, share, 0)
        top_logit = jnp.max(logits, axis=1, keepdims=True)
        shifted = jnp.exp(logits - top_logit)
        row_total = jnp.sum(shifted, axis=1, keepdims=True)
        log_total = top_logit[:, 0] + jnp.log(row_total[:, 0])
        classes = lax.broadcasted_iota(jnp.int32, logits.shape, 1)
        onehot = (classes == labels_part[:, None]).astype(jnp.float32)
        loss_part = jnp.sum(log_total - jnp.sum(onehot * logits, axis=1)) / tokens
        dz_part = ((shifted / row_total - onehot) / tokens).astype(jnp.bfloat16)
        dlogits = jnp.zeros((ways, share, padded), jnp.bfloat16)
        for step, item in xor_blocks(dz_part, bits).items():
            dlogits = put(dlogits, item, mine ^ step)
        return pre, out, dlogits.reshape(half, padded), loss_part

    both = [half_forward(number) for number in (0, 1)]
    pre_seven, out_seven, dlogits = (
        jnp.concatenate([item[spot] for item in both]) for spot in range(3)
    )
    loss_part = both[0][3] + both[1][3]
    hidden = jnp.concatenate(hiddens)

    delta_seven = layer_delta(pre_seven, against_rows(dlogits, kept_eight))

    def upstream(delta, step):
        return against_rows(delta, kept_seven[step * width : (step + 1) * width])

    top_bit = bits[0]
    cuts = [0, batch_rows // 64 * 22, batch_rows // 64 * 43, batch_rows]

    def near_sums(first, delta):
        ups = {step: upstream(delta, step) for step in range(first, first + top_bit)}
        for bit in reversed(bits[1:]):
            for step in range(first, first + top_bit, 2 * bit):
                ups[step] = ups[step] + swap(ups[step + bit], "mp", bit)
        return ups[first]

    crossing = near_sums(top_bit, delta_seven)
    grad_eight = contract_rows(out_seven, dlogits)
    limit_eight, peak_eight = grad_limits(grad_eight, outs)
    crossing, grad_eight, limit_eight, peak_eight, delta_seven, dlogits = settle(
        crossing, grad_eight, limit_eight, peak_eight, delta_seven, dlogits
    )
    crossing = [crossing[low:high] for low, high in zip(cuts[:-1], cuts[1:])]
    grad_seven = contract_rows(hidden, delta_seven)
    limit_seven, peak_seven = grad_limits(grad_seven, width)
    tops = fold(jnp.stack([peak_eight, peak_seven]), jnp.maximum, ("dp",))
    crossing, grad_seven, limit_seven, tops, delta_seven = settle(
        crossing, grad_seven, limit_seven, tops, delta_seven
    )
    top_eight, top_seven = tops[0], tops[1]

    def cross(step):
        def work(carried):
            delta, crossing, crossed, own_up = carried
            if step == 0:
                own_up = near_sums(0, delta)
            return (delta, crossing, crossed + [swap(crossing[step], "mp", top_bit)], own_up)

        return work

    def grad_fc_six(carried):
        _, _, crossed, own_up = carried
        delta_six = layer_delta(pre_six, own_up + jnp.concatenate(crossed))
        grad_six = contract_rows(inputs, delta_six)
        limit_six, peak_six = grad_limits(grad_six, width)
        return (delta_six, grad_six, limit_six, peak_six)

    def sum_or_max(one, two):
        return jnp.concatenate([one[:-1] + two[:-1], jnp.maximum(one[-1:], two[-1:])])

    def small_sums(carried):
        delta_six, grad_six, limit_six, peak_six = carried
        columns = [
            jnp.sum(item.astype(jnp.float32), axis=0) for item in (delta_six, delta_seven, dlogits)
        ]
        small = fold(jnp.concatenate(columns + [peak_six[None]]), sum_or_max, ("dp",))
        return (grad_six, limit_six, small)

    beside = [
        cross(0),
        cross(1),
        cross(2),
        grad_fc_six,
    ]
    (reduced_eight, reduced_seven), carried = scatter(
        [grad_eight.reshape(replicas, rows_eight, padded), grad_seven.reshape(replicas, rows_seven, width)],
        [limit_eight, limit_seven],
        [top_eight, top_seven],
        [noise_wide.reshape(replicas, rows_eight, padded), noise_seven.reshape(replicas, rows_seven, width)],
        [None, group_seven],
        [0, 0],
        False,
        beside,
        (delta_seven, crossing, [], None),
    )
    grad_six, limit_six, small = small_sums(carried)
    top_six = small[-1]
    (reduced_six,), (reduced_seven, reduced_eight) = scatter(
        [grad_six.reshape(replicas, rows_six, width)],
        [limit_six],
        [top_six],
        [noise_six.reshape(replicas, rows_six, width)],
        [group_six],
        [near_six],
        False,
        [same] * rings + [lambda carried: (carried[0], carried[1].T)],
        (reduced_seven, reduced_eight[:, :outs]),
    )
    grad_pair = small[: 2 * width].reshape(2, width)
    grad_out = small[2 * width : 2 * width + outs]
    squares = (
        jnp.sum(reduced_six * reduced_six)
        + jnp.sum(reduced_seven * reduced_seven)
        + jnp.sum(reduced_eight * reduced_eight)
        + jnp.sum(grad_pair * grad_pair) / replicas
        + jnp.sum(grad_out * grad_out) / (replicas * ways)
    )
    totals = fold(jnp.stack([squares, loss_part]), jnp.add, ("dp", "mp"))
    total_squares, loss = totals[0], totals[1]
    grad_norm = jnp.sqrt(total_squares)
    factor = clip_norm / jnp.maximum(grad_norm, clip_norm)
    new_six, new_m_six, new_v_six = adam_step(
        w_six, m_six, v_six, factor * reduced_six, decay_rate, learn_rate
    )
    new_seven, new_m_seven, new_v_seven = adam_step(
        w_seven, m_seven, v_seven, factor * reduced_seven, decay_rate, learn_rate
    )
    new_eight, new_m_eight, new_v_eight = (
        item.T
        for item in adam_step(
            w_eight.T, m_eight.T, v_eight.T, factor * reduced_eight, decay_rate, learn_rate
        )
    )
    new_biases, new_m_biases, new_v_biases = adam_step(
        biases, m_biases, v_biases, factor * grad_pair, 0.0, bias_rate
    )
    new_bias_out, new_m_bias_out, new_v_bias_out = adam_step(
        bias_out, m_bias_out, v_bias_out, factor * grad_out, 0.0, bias_rate
    )
    return (
        loss,
        grad_norm,
        new_six,
        new_seven,
        new_eight,
        new_m_six,
        new_m_seven,
        new_m_eight,
        new_v_six,
        new_v_seven,
        new_v_eight,
        new_six.astype(jnp.bfloat16),
        new_seven.astype(jnp.bfloat16),
        new_eight.astype(jnp.bfloat16),
        new_biases,
        new_bias_out,
        new_m_biases,
        new_v_biases,
        new_m_bias_out,
        new_v_bias_out,
    )


def solution(mesh):
    return jax.shard_map(
        shards,
        mesh=mesh,
        in_specs=(
            P("dp", "mp"),
            P("dp"),
            P("dp", "mp"),
            P("dp", "mp"),
            P(("dp", "mp"), None),
            P("dp", "mp"),
            P("dp", "mp"),
            P(("mp", "dp"), None),
            P("dp", "mp"),
            P("dp", "mp"),
            P(("mp", "dp"), None),
            P("dp", "mp"),
            P("dp", "mp"),
            P(("mp", "dp"), None),
            P(None, "mp"),
            P(),
            P(None, "mp"),
            P(None, "mp"),
            P(),
            P(),
        ),
        out_specs=(
            P(),
            P(),
            P("dp", "mp"),
            P("dp", "mp"),
            P(("mp", "dp"), None),
            P("dp", "mp"),
            P("dp", "mp"),
            P(("mp", "dp"), None),
            P("dp", "mp"),
            P("dp", "mp"),
            P(("mp", "dp"), None),
            P("dp", "mp"),
            P("dp", "mp"),
            P(("mp", "dp"), None),
            P(None, "mp"),
            P(),
            P(None, "mp"),
            P(None, "mp"),
            P(),
            P(),
        ),
        check_vma=False,
    )
```

```python
import jax
import jax.numpy as jnp
from jax import lax
from jax.sharding import PartitionSpec as P

STEP = 3


beta_one = 0.5
beta_two = 0.5
learn_rate = 0.01
bias_rate = 0.05
decay_rate = 0.1
adam_eps = 1e-08
clip_norm = 0.05
tiny_eps = 1e-12


def matmul(left, right):
    return jnp.dot(left, right, preferred_element_type=jnp.float32)


def contract_rows(left, right):
    return lax.dot_general(
        left, right, (((0,), (0,)), ((), ())), preferred_element_type=jnp.float32
    )


def against_rows(left, right):
    return lax.dot_general(
        left, right, (((1,), (1,)), ((), ())), preferred_element_type=jnp.float32
    )


def layer_forward(pre_sum, bias_row):
    pre_act = pre_sum + bias_row
    return (pre_act, jax.nn.silu(pre_act).astype(jnp.bfloat16))


def layer_delta(pre_act, upstream):
    sigmoid_val = jax.nn.sigmoid(pre_act)
    slope = sigmoid_val * (1.0 + pre_act * (1.0 - sigmoid_val))
    return (upstream * slope).astype(jnp.bfloat16)


def grad_limits(grad_block, columns):
    squares = jnp.sum(grad_block * grad_block)
    limit = 2.5 * jnp.sqrt(squares / (grad_block.shape[0] * columns))
    return (limit, jnp.minimum(jnp.max(jnp.abs(grad_block)), limit))


def swap(value, axis, bit):
    size = lax.axis_size(axis)
    return lax.ppermute(value, axis, [(i, i ^ bit) for i in range(size)])


def turn(value):
    size = lax.axis_size("dp")
    return lax.ppermute(value, "dp", [(i, (i + 2) % size) for i in range(size)])


def spread_bits(axis):
    bit = 1
    while bit < lax.axis_size(axis):
        yield bit
        bit *= 2


def fold(value, combine, axes):
    for axis in axes:
        for bit in spread_bits(axis):
            value = combine(value, swap(value, axis, bit))
    return value


def settle(*values):
    return lax.optimization_barrier(values)


def owner(step, flip):
    size = lax.axis_size("dp")
    here = lax.axis_index("dp")
    return ((here + size - 2 * step) % size) ^ flip


def place(index, blocks):
    if blocks is None:
        return index
    mine = lax.axis_index("mp")
    return ((index // blocks) ^ mine) * blocks + index % blocks


def put(whole, piece, index, row=0):
    return lax.dynamic_update_slice(whole, piece[None], (index, row, 0))


def take(whole, index, row, rows):
    return lax.dynamic_slice(whole, (index, row, 0), (1, rows, whole.shape[2]))[0]


def xor_blocks(value, bits):
    blocks = {0: value}
    for bit in bits:
        blocks |= {step ^ bit: swap(item, "mp", bit) for step, item in blocks.items()}
    return blocks


def near_rows(rows, rings):
    return max(16, (rows // (2 * rings + 2) + 8) // 16 * 16)


def reorder(whole, group):
    if group is None:
        return whole
    mine = lax.axis_index("mp")
    ways = whole.shape[0] // group
    grouped = whole.reshape(ways, group, *whole.shape[1:])
    return jnp.concatenate(
        [lax.dynamic_index_in_dim(grouped, mine ^ step, 0, keepdims=False) for step in range(ways)]
    )


def overlaps(sizes, row, count):
    start = 0
    for spot, size in enumerate(sizes):
        low, high = max(row, start), min(row + count, start + size)
        if low < high:
            yield spot, low - start, high - low, low - row
        start += size


def soft_ternary(grad_block, limit, peak_val, noise_val):
    clipped = jnp.clip(grad_block, -limit, limit)
    ratio = clipped / (peak_val + tiny_eps)
    value = jnp.clip(4.0 * ratio, -1.0, 1.0) * jnp.clip(
        2.0 * (jnp.abs(ratio) - noise_val.astype(jnp.float32)) + 0.5, 0.0, 1.0
    )
    return value.astype(jnp.bfloat16)


def adam_step(weight, moment, second, grad_val, decay, rate):
    moment_new = beta_one * moment + (1.0 - beta_one) * grad_val
    second_new = beta_two * second + (1.0 - beta_two) * grad_val * grad_val
    first_fix = 1.0 - beta_one**STEP
    second_fix = 1.0 - beta_two**STEP
    weight_new = weight - rate * (
        moment_new / first_fix / (jnp.sqrt(second_new / second_fix) + adam_eps) + decay * weight
    )
    return (weight_new, moment_new, second_new)


LONG_RING = 8


def spans_of(rows, count):
    marks = [rows * i // count // 16 * 16 for i in range(count)] + [rows]
    return list(zip(marks[:-1], marks[1:]))


def same(carried):
    return carried


def gather_whole(shard, group):
    return reorder(lax.all_gather(shard, "dp", axis=0), group)


def gather_queue(first, second, groups, near, hooks, carried):
    rings = lax.axis_size("dp") // 2
    rows = first.shape[0]
    middle = rows // 32 * 16
    sizes = [shard.shape[0] for shard in second]
    joined = jnp.concatenate(second)
    cut = joined.shape[0] - near
    ready = {
        ("a", 0): first[:middle],
        ("b", 0): first[middle:],
        ("f", 0): joined[:cut],
        ("n",): joined[cut:],
    }
    z_tasks = [(name, hop) for hop in range(rings - 1) for name in "ab"]
    z_tasks += [(name, hop) for hop in range(rings - 1) for name in "fp"]
    y_tasks = [(name, hop) for hop in range(rings) for name in "ab"]
    y_tasks += [("f", hop) for hop in range(rings)]

    def store(wholes, piece, step, flip, row):
        wholes = list(wholes)
        for spot, inner, count, outer in overlaps(sizes, row, piece.shape[0]):
            index = place(owner(step, flip), groups[1][spot])
            wholes[1 + spot] = put(wholes[1 + spot], piece[outer : outer + count], index, inner)
        return wholes

    def store_first(wholes, piece, step, flip, row):
        index = place(owner(step, flip), groups[0])
        return [put(wholes[0], piece, index, row)] + list(wholes[1:])

    wholes = None
    flight, pending, last = {}, None, {}
    step = 0
    while z_tasks or y_tasks or flight:
        started = {}
        if z_tasks and z_tasks[0] in ready:
            name, hop = z_tasks.pop(0)
            started["z", name, hop + 1] = turn(ready[name, hop])
        if y_tasks and y_tasks[0] in ready:
            name, hop = y_tasks.pop(0)
            started["y", name, hop] = swap(ready[name, hop], "dp", 1)
            if (name, hop) == ("b", rings - 2):
                started["y", "n", 0] = swap(ready["n",], "dp", 1)
        if step == 1:
            wholes = [jnp.zeros((2 * rings, *item.shape), item.dtype) for item in (first, *second)]
            wholes = store_first(wholes, ready["a", 0], 0, 0, 0)
            wholes = store_first(wholes, ready["b", 0], 0, 0, middle)
        if step == 2:
            wholes = store(wholes, ready["f", 0], 0, 0, 0)
            wholes = store(wholes, ready["n",], 0, 0, cut)
        later = None
        if step in hooks:
            carried, later = hooks[step](carried, wholes, last)
        flight, ready, wholes, carried, pending, last = settle(
            flight, ready, wholes, carried, pending, last
        )
        if pending is not None:
            carried = carried | pending
        pending = later
        for (axis, name, hop), piece in flight.items():
            if name in "ab":
                row = 0 if name == "a" else middle
                if axis == "y" and hop == rings - 1:
                    last[name] = piece
                else:
                    wholes = store_first(wholes, piece, hop, int(axis == "y"), row)
            elif name == "f":
                wholes = store(wholes, piece, hop, int(axis == "y"), 0)
                if axis == "y" and hop == rings - 1:
                    last[name] = piece
            elif name == "n":
                wholes = store(wholes, piece, 0, 1, cut)
                ready["p", 0] = jnp.concatenate([ready["n",], piece])
            else:
                if hop == rings - 1:
                    last[name] = piece
                for flip in (0, 1):
                    wholes = store(wholes, piece[flip * near : (flip + 1) * near], hop, flip, cut)
            if axis == "z":
                ready[name, hop] = piece
        flight = started
        step += 1
    return wholes, last, carried | (pending or {})


def scatter(grads, limits, tops, noises, groups, nears, ahead, beside, carried):
    rings = lax.axis_size("dp") // 2
    if rings > LONG_RING:
        for work in beside:
            carried = work(carried)
        results = []
        for grad, limit, top, noise, group in zip(grads, limits, tops, noises, groups):
            tern = soft_ternary(reorder(grad, group), limit, top, noise)
            total = lax.psum_scatter(tern.astype(jnp.float32), "dp", scatter_dimension=0)
            results.append(top * total)
        return results, carried
    beside = beside + [same] * (2 * rings - len(beside))
    spots = range(len(grads))
    cuts = [grad.shape[1] - near for grad, near in zip(grads, nears)]
    hops = rings - 1 if any(nears) else 1
    cutting = [
        spans_of(cut, hops) if near else [(0, cut)] + [None] * (hops - 1)
        for cut, near in zip(cuts, nears)
    ]

    ready = [
        soft_ternary(grad, limit, top, noise) if group is None else None
        for grad, limit, top, noise, group in zip(grads, limits, tops, noises, groups)
    ]

    def tern(spot, step, flip, row, count):
        index = owner(step, flip)
        if ready[spot] is not None:
            return take(ready[spot], index, row, count)
        return soft_ternary(
            take(grads[spot], place(index, groups[spot]), row, count),
            limits[spot],
            tops[spot],
            take(noises[spot], index, row, count),
        )

    def terns(step, flip, spans):
        return [
            None if span is None else tern(spot, step, flip, span[0], span[1] - span[0])
            for spot, span in zip(spots, spans)
        ]

    def far_terns(step, flip):
        return terns(step, flip, [(0, cut) for cut in cuts])

    def near_terns(step):
        return [
            jnp.concatenate([tern(spot, step, flip, cuts[spot], nears[spot]) for flip in (0, 1)])
            if nears[spot]
            else None
            for spot in spots
        ]

    def each(work, *lists):
        return [None if items[0] is None else work(*items) for items in zip(*lists)]

    def wide(value):
        return value.astype(jnp.float32)

    def narrow(value):
        return value.astype(jnp.bfloat16)

    def across(value):
        return swap(value, "dp", 1)

    order = list(range(1, rings)) + [0]
    pairs = near_terns(order[0])
    sending = [terns(order[0], 1, [cut[0] for cut in cutting])]
    limits, carried = settle(limits, carried)
    aways, owns = {}, {}
    got = [[] for spot in spots]
    for hop in range(1, hops + 1):
        others = each(across, sending[hop - 1])
        arrived = each(lambda item: turn(narrow(item)), pairs)
        more = near_terns(order[hop])
        if hop < hops:
            sending.append(terns(order[0], 1, [cut[hop] for cut in cutting]))
        if hop == 1:
            owns[0] = far_terns(order[0], 0)
        if hop == hops:
            aways[1] = far_terns(order[1], 1)
        carried = beside[hop - 1](carried)
        others, arrived, more, sending, aways, owns, limits, carried = settle(
            others, arrived, more, sending, aways, owns, limits, carried
        )
        pairs = each(lambda item, add: wide(item) + wide(add), arrived, more)
        for spot in spots:
            if others[spot] is not None:
                got[spot].append(others[spot])
    sums = [wide(owns[0][spot]) + wide(jnp.concatenate(got[spot])) for spot in spots]
    for spin in range(1, rings):
        others = each(across, aways[spin])
        moved = each(lambda item: turn(narrow(item)), sums)
        lasts = None
        if spin == rings - 1:
            lasts = [
                item if item is None else across(narrow(item[near:]))
                for item, near in zip(pairs, nears)
            ]
        for later in range(spin, rings if ahead else spin + 1):
            if later not in owns:
                owns[later] = far_terns(order[later], 0)
        for later in range(spin + 1, rings if ahead else min(spin + 2, rings)):
            if later not in aways:
                aways[later] = far_terns(order[later], 1)
        carried = beside[hops - 1 + spin](carried)
        others, moved, lasts, pairs, aways, owns, limits, carried = settle(
            others, moved, lasts, pairs, aways, owns, limits, carried
        )
        sums = each(
            lambda own, item, more: wide(own) + wide(item) + wide(more), owns[spin], others, moved
        )
    results = []
    for spot, near in zip(spots, nears):
        total = sums[spot]
        if near:
            total = jnp.concatenate([total, pairs[spot][:near] + wide(lasts[spot])])
        results.append(tops[spot] * total)
    return results, carried


def shards(
    features,
    labels,
    noise_six,
    noise_seven,
    noise_eight,
    w_six,
    w_seven,
    w_eight,
    m_six,
    m_seven,
    m_eight,
    v_six,
    v_seven,
    v_eight,
    biases,
    bias_out,
    m_biases,
    v_biases,
    m_bias_out,
    v_bias_out,
):
    mine = lax.axis_index("mp")
    replicas = lax.axis_size("dp")
    ways = lax.axis_size("mp")
    rings = replicas // 2
    batch_rows = features.shape[0]
    tokens = batch_rows * replicas
    half = batch_rows // 2
    width = biases.shape[1]
    outs = bias_out.shape[0]
    padded = outs + -outs % 128
    rows_six, rows_seven, rows_eight = w_six.shape[0], w_seven.shape[0], w_eight.shape[0]
    group_six, group_seven = features.shape[1] // rows_six, width // rows_seven
    near_six = near_rows(rows_six, rings)
    bits = list(reversed(list(spread_bits("mp"))))
    far_bits, near_bit = bits[:-1], bits[-1]

    def widen(value):
        return jnp.pad(value, ((0, 0), (0, padded - outs)))

    def halves(value):
        return [value[:half], value[half:]]

    def over_far(own):
        done = xor_blocks(own, far_bits)
        del done[0]
        return done

    def over_near(blocks):
        return {step ^ near_bit: swap(item, "mp", near_bit) for step, item in blocks.items()}

    def join(halves_of_blocks):
        return jnp.concatenate(
            [
                jnp.concatenate([blocks[step] for step in range(ways)], axis=1)
                for blocks in halves_of_blocks
            ]
        )

    far_features = over_far(features)
    shards_cast = [
        w_six.astype(jnp.bfloat16),
        widen(w_eight.astype(jnp.bfloat16)),
        w_seven.astype(jnp.bfloat16),
    ]
    if rings > LONG_RING:
        inputs = join([{0: features} | far_features | over_near({0: features} | far_features)])
        noise_wide = widen(noise_eight)
        kept_six = gather_whole(shards_cast[0], group_six).reshape(-1, width)
        kept_eight = gather_whole(shards_cast[1], None)
        kept_seven = gather_whole(shards_cast[2], group_seven)
        pre_six, out_six = layer_forward(matmul(inputs, kept_six), biases[0])
        hidden_blocks = []
        for item in halves(out_six):
            blocks = {0: item} | over_far(item)
            hidden_blocks.append(blocks | over_near(blocks))
        hiddens = [join([blocks]) for blocks in hidden_blocks]

        def sum_seven(number):
            return matmul(hiddens[number], kept_seven.reshape(-1, width))

    else:
        count = 2 * rings

        def own_near(carried, wholes, last):
            return {"near": swap(features, "mp", near_bit), "noise": widen(noise_eight)}, None

        def far_there(carried, wholes, last):
            return carried | {"far": far_features}, None

        def far_near(carried, wholes, last):
            return carried | {"both": over_near(carried["far"])}, None

        def join_inputs(carried, wholes, last):
            blocks = {0: features, near_bit: carried["near"]} | carried["far"] | carried["both"]
            return {"inputs": join([blocks]), "noise": carried["noise"]}, None

        def fc_six_most(carried, wholes, last):
            early = matmul(carried["inputs"], wholes[0].reshape(-1, width))
            return carried, {"early": early}

        def fc_six_rest(carried, wholes, last):
            start = place(owner(rings - 1, 1), group_six) * rows_six
            columns = lax.dynamic_slice_in_dim(carried["inputs"], start, rows_six, 1)
            rest = matmul(columns, jnp.concatenate([last["a"], last["b"]]))
            pre_six, out_six = layer_forward(carried["early"] + rest, biases[0])
            one, two = halves(out_six)
            crossing["one"], crossing["two"] = over_far(one), over_far(two)
            return (
                {"inputs": carried["inputs"], "noise": carried["noise"], "pre": pre_six, "out": (one, two)},
                None,
            )

        crossing = {}

        def hidden_own(carried, wholes, last):
            own = [over_near({0: item}) for item in carried["out"]]
            return carried | {"own": own}, None

        def hidden_one(carried, wholes, last):
            return carried | {"one": crossing["one"]}, None

        def hidden_one_near(carried, wholes, last):
            blocks = {0: carried["out"][0]} | carried["own"][0] | carried["one"]
            hidden = join([blocks | over_near(carried["one"])])
            early = matmul(hidden, wholes[2].reshape(-1, width))
            return carried, {"hidden_one": hidden, "early_one": early}

        def fc_seven_most(carried, wholes, last):
            far = crossing["two"]
            two = join([{0: carried["out"][1]} | carried["own"][1] | far | over_near(far)])
            names = ("inputs", "noise", "pre")
            return {name: carried[name] for name in names} | {"hidden_two": two}, None

        hooks = {
            1: own_near,
            count - 4: far_there,
            count - 3: far_near,
            count - 2: join_inputs,
            count - 1: fc_six_most,
            count + 1: fc_six_rest,
            count + 2: hidden_own,
            count + 3: hidden_one,
            count + 4: hidden_one_near,
            count + 5: fc_seven_most,
        }
        near = (rows_six + rows_seven + rows_eight) // (2 * rings - 2) // 16 * 16
        (_, kept_eight, kept_seven), last, carried = gather_queue(
            shards_cast[0],
            shards_cast[1:],
            [group_six, [None, group_seven]],
            min(near, rows_seven // 32 * 16),
            hooks,
            {},
        )
        inputs, noise_wide, pre_six = carried["inputs"], carried["noise"], carried["pre"]
        hiddens = [carried["hidden_one"], carried["hidden_two"]]
        start = place(owner(rings - 1, 1), group_seven) * rows_seven
        other_start = place(owner(rings - 1, 0), group_seven) * rows_seven
        rest = last["f"][rows_eight:]
        count, most = last["p"].shape[0] // 2, rest.shape[0]

        def columns(number, low, size):
            return lax.dynamic_slice_in_dim(hiddens[number], low, size, 1)

        def sum_seven(number):
            if number == 1:
                return matmul(hiddens[1], kept_seven)
            whole_block = jnp.concatenate([rest, last["p"][count:]])
            return (
                carried["early_one"]
                + matmul(columns(0, start, rows_seven), whole_block)
                + matmul(columns(0, other_start + most, count), last["p"][:count])
            )

    kept_seven, kept_eight = kept_seven.reshape(-1, width), kept_eight.reshape(-1, padded)

    bias_wide = jnp.pad(bias_out, (0, padded - outs), constant_values=-1e30)
    share = half // ways

    def half_forward(number, earlier):
        pre, out = layer_forward(sum_seven(number), biases[1])
        if earlier is not None:
            pre, out, earlier = settle(pre, out, earlier)
        shares = out.reshape(ways, share, width)
        parts = {
            step: matmul(lax.dynamic_index_in_dim(shares, mine ^ step, 0, keepdims=False), kept_eight)
            for step in range(ways)
        }
        for bit in reversed(bits):
            for step in range(0, ways, 2 * bit):
                parts[step] = parts[step] + swap(parts[step + bit], "mp", bit)
        logits = parts[0] + bias_wide
        labels_part = lax.dynamic_slice_in_dim(labels, number * half + mine * share, share, 0)
        top_logit = jnp.max(logits, axis=1, keepdims=True)
        shifted = jnp.exp(logits - top_logit)
        row_total = jnp.sum(shifted, axis=1, keepdims=True)
        log_total = top_logit[:, 0] + jnp.log(row_total[:, 0])
        classes = lax.broadcasted_iota(jnp.int32, logits.shape, 1)
        onehot = (classes == labels_part[:, None]).astype(jnp.float32)
        loss_part = jnp.sum(log_total - jnp.sum(onehot * logits, axis=1)) / tokens
        dz_part = ((shifted / row_total - onehot) / tokens).astype(jnp.bfloat16)
        dlogits = jnp.zeros((ways, share, padded), jnp.bfloat16)
        for step, item in xor_blocks(dz_part, bits).items():
            dlogits = put(dlogits, item, mine ^ step)
        return pre, out, dlogits.reshape(half, padded), loss_part, logits

    both = [half_forward(0, None)]
    both.append(half_forward(1, both[0][4]))
    dlogits = jnp.concatenate([item[2] for item in both])
    pre_seven, out_seven, _ = settle(
        [item[0] for item in both], [item[1] for item in both], both[0][4][:8, :128]
    )
    pre_seven, out_seven = jnp.concatenate(pre_seven), jnp.concatenate(out_seven)
    pre_seven, out_seven, dlogits = settle(pre_seven, out_seven, dlogits)
    loss_part = both[0][3] + both[1][3]
    hidden = jnp.concatenate(hiddens)

    delta_seven = layer_delta(pre_seven, against_rows(dlogits, kept_eight))

    def upstream(delta, step):
        return against_rows(delta, kept_seven[step * width : (step + 1) * width])

    top_bit = bits[0]
    cuts = [0, batch_rows // 64 * 22, batch_rows // 64 * 43, batch_rows]

    def near_sums(first, delta):
        ups = {step: upstream(delta, step) for step in range(first, first + top_bit)}
        for bit in reversed(bits[1:]):
            for step in range(first, first + top_bit, 2 * bit):
                ups[step] = ups[step] + swap(ups[step + bit], "mp", bit)
        return ups[first]

    crossing = near_sums(top_bit, delta_seven)
    grad_eight = contract_rows(out_seven, dlogits)
    limit_eight, peak_eight = grad_limits(grad_eight, outs)
    crossing, grad_eight, limit_eight, peak_eight, delta_seven, dlogits = settle(
        crossing, grad_eight, limit_eight, peak_eight, delta_seven, dlogits
    )
    crossing = [crossing[low:high] for low, high in zip(cuts[:-1], cuts[1:])]
    grad_seven = contract_rows(hidden, delta_seven)
    limit_seven, peak_seven = grad_limits(grad_seven, width)
    tops = fold(jnp.stack([peak_eight, peak_seven]), jnp.maximum, ("dp",))
    crossing, grad_seven, limit_seven, tops, delta_seven = settle(
        crossing, grad_seven, limit_seven, tops, delta_seven
    )
    top_eight, top_seven = tops[0], tops[1]

    def cross(step):
        def work(carried):
            delta, crossing, crossed, own_up = carried
            if step == 0:
                own_up = near_sums(0, delta)
            return (delta, crossing, crossed + [swap(crossing[step], "mp", top_bit)], own_up)

        return work

    def grad_fc_six(carried):
        _, _, crossed, own_up = carried
        delta_six = layer_delta(pre_six, own_up + jnp.concatenate(crossed))
        grad_six = contract_rows(inputs, delta_six)
        limit_six, peak_six = grad_limits(grad_six, width)
        return (delta_six, grad_six, limit_six, peak_six)

    def sum_or_max(one, two):
        return jnp.concatenate([one[:-1] + two[:-1], jnp.maximum(one[-1:], two[-1:])])

    def small_sums(carried):
        delta_six, grad_six, limit_six, peak_six = carried
        columns = [
            jnp.sum(item.astype(jnp.float32), axis=0) for item in (delta_six, delta_seven, dlogits)
        ]
        small = fold(jnp.concatenate(columns + [peak_six[None]]), sum_or_max, ("dp",))
        return (grad_six, limit_six, small)

    beside = [
        cross(0),
        cross(1),
        cross(2),
        grad_fc_six,
    ]
    (reduced_eight, reduced_seven), carried = scatter(
        [grad_eight.reshape(replicas, rows_eight, padded), grad_seven.reshape(replicas, rows_seven, width)],
        [limit_eight, limit_seven],
        [top_eight, top_seven],
        [noise_wide.reshape(replicas, rows_eight, padded), noise_seven.reshape(replicas, rows_seven, width)],
        [None, group_seven],
        [0, 0],
        False,
        beside,
        (delta_seven, crossing, [], None),
    )
    grad_six, limit_six, small = small_sums(carried)
    top_six = small[-1]
    (reduced_six,), (reduced_seven, reduced_eight) = scatter(
        [grad_six.reshape(replicas, rows_six, width)],
        [limit_six],
        [top_six],
        [noise_six.reshape(replicas, rows_six, width)],
        [group_six],
        [near_six],
        False,
        [same] * rings + [lambda carried: (carried[0], carried[1].T)],
        (reduced_seven, reduced_eight[:, :outs]),
    )
    grad_pair = small[: 2 * width].reshape(2, width)
    grad_out = small[2 * width : 2 * width + outs]
    squares = (
        jnp.sum(reduced_six * reduced_six)
        + jnp.sum(reduced_seven * reduced_seven)
        + jnp.sum(reduced_eight * reduced_eight)
        + jnp.sum(grad_pair * grad_pair) / replicas
        + jnp.sum(grad_out * grad_out) / (replicas * ways)
    )
    totals = fold(jnp.stack([squares, loss_part]), jnp.add, ("dp", "mp"))
    total_squares, loss = totals[0], totals[1]
    grad_norm = jnp.sqrt(total_squares)
    factor = clip_norm / jnp.maximum(grad_norm, clip_norm)
    new_six, new_m_six, new_v_six = adam_step(
        w_six, m_six, v_six, factor * reduced_six, decay_rate, learn_rate
    )
    new_seven, new_m_seven, new_v_seven = adam_step(
        w_seven, m_seven, v_seven, factor * reduced_seven, decay_rate, learn_rate
    )
    new_eight, new_m_eight, new_v_eight = (
        item.T
        for item in adam_step(
            w_eight.T, m_eight.T, v_eight.T, factor * reduced_eight, decay_rate, learn_rate
        )
    )
    new_biases, new_m_biases, new_v_biases = adam_step(
        biases, m_biases, v_biases, factor * grad_pair, 0.0, bias_rate
    )
    new_bias_out, new_m_bias_out, new_v_bias_out = adam_step(
        bias_out, m_bias_out, v_bias_out, factor * grad_out, 0.0, bias_rate
    )
    return (
        loss,
        grad_norm,
        new_six,
        new_seven,
        new_eight,
        new_m_six,
        new_m_seven,
        new_m_eight,
        new_v_six,
        new_v_seven,
        new_v_eight,
        new_six.astype(jnp.bfloat16),
        new_seven.astype(jnp.bfloat16),
        new_eight.astype(jnp.bfloat16),
        new_biases,
        new_bias_out,
        new_m_biases,
        new_v_biases,
        new_m_bias_out,
        new_v_bias_out,
    )


def solution(mesh):
    return jax.shard_map(
        shards,
        mesh=mesh,
        in_specs=(
            P("dp", "mp"),
            P("dp"),
            P("dp", "mp"),
            P("dp", "mp"),
            P(("dp", "mp"), None),
            P("dp", "mp"),
            P("dp", "mp"),
            P(("mp", "dp"), None),
            P("dp", "mp"),
            P("dp", "mp"),
            P(("mp", "dp"), None),
            P("dp", "mp"),
            P("dp", "mp"),
            P(("mp", "dp"), None),
            P(None, "mp"),
            P(),
            P(None, "mp"),
            P(None, "mp"),
            P(),
            P(),
        ),
        out_specs=(
            P(),
            P(),
            P("dp", "mp"),
            P("dp", "mp"),
            P(("mp", "dp"), None),
            P("dp", "mp"),
            P("dp", "mp"),
            P(("mp", "dp"), None),
            P("dp", "mp"),
            P("dp", "mp"),
            P(("mp", "dp"), None),
            P("dp", "mp"),
            P("dp", "mp"),
            P(("mp", "dp"), None),
            P(None, "mp"),
            P(),
            P(None, "mp"),
            P(None, "mp"),
            P(),
            P(),
        ),
        check_vma=False,
    )
```

```python
import jax
import jax.numpy as jnp
from jax import lax
from jax.sharding import PartitionSpec as P

STEP = 3


beta_one = 0.5
beta_two = 0.5
learn_rate = 0.01
bias_rate = 0.05
decay_rate = 0.1
adam_eps = 1e-08
clip_norm = 0.05
tiny_eps = 1e-12


def matmul(left, right):
    return jnp.dot(left, right, preferred_element_type=jnp.float32)


def contract_rows(left, right):
    return lax.dot_general(
        left, right, (((0,), (0,)), ((), ())), preferred_element_type=jnp.float32
    )


def against_rows(left, right):
    return lax.dot_general(
        left, right, (((1,), (1,)), ((), ())), preferred_element_type=jnp.float32
    )


def layer_forward(pre_sum, bias_row):
    pre_act = pre_sum + bias_row
    return (pre_act, jax.nn.silu(pre_act).astype(jnp.bfloat16))


def layer_delta(pre_act, upstream):
    sigmoid_val = jax.nn.sigmoid(pre_act)
    slope = sigmoid_val * (1.0 + pre_act * (1.0 - sigmoid_val))
    return (upstream * slope).astype(jnp.bfloat16)


def grad_limits(grad_block, columns):
    squares = jnp.sum(grad_block * grad_block)
    limit = 2.5 * jnp.sqrt(squares / (grad_block.shape[0] * columns))
    return (limit, jnp.minimum(jnp.max(jnp.abs(grad_block)), limit))


def swap(value, axis, bit):
    size = lax.axis_size(axis)
    return lax.ppermute(value, axis, [(i, i ^ bit) for i in range(size)])


def turn(value):
    size = lax.axis_size("dp")
    return lax.ppermute(value, "dp", [(i, (i + 2) % size) for i in range(size)])


def spread_bits(axis):
    bit = 1
    while bit < lax.axis_size(axis):
        yield bit
        bit *= 2


def fold(value, combine, axes):
    for axis in axes:
        for bit in spread_bits(axis):
            value = combine(value, swap(value, axis, bit))
    return value


def settle(*values):
    return lax.optimization_barrier(values)


def owner(step, flip):
    size = lax.axis_size("dp")
    here = lax.axis_index("dp")
    return ((here + size - 2 * step) % size) ^ flip


def place(index, blocks):
    if blocks is None:
        return index
    mine = lax.axis_index("mp")
    return ((index // blocks) ^ mine) * blocks + index % blocks


def put(whole, piece, index, row=0):
    return lax.dynamic_update_slice(whole, piece[None], (index, row, 0))


def take(whole, index, row, rows):
    return lax.dynamic_slice(whole, (index, row, 0), (1, rows, whole.shape[2]))[0]


def xor_blocks(value, bits):
    blocks = {0: value}
    for bit in bits:
        blocks |= {step ^ bit: swap(item, "mp", bit) for step, item in blocks.items()}
    return blocks


def near_rows(rows, rings):
    return max(16, (rows // (2 * rings + 2) + 8) // 16 * 16)


def reorder(whole, group):
    if group is None:
        return whole
    mine = lax.axis_index("mp")
    ways = whole.shape[0] // group
    grouped = whole.reshape(ways, group, *whole.shape[1:])
    return jnp.concatenate(
        [lax.dynamic_index_in_dim(grouped, mine ^ step, 0, keepdims=False) for step in range(ways)]
    )


def overlaps(sizes, row, count):
    start = 0
    for spot, size in enumerate(sizes):
        low, high = max(row, start), min(row + count, start + size)
        if low < high:
            yield spot, low - start, high - low, low - row
        start += size


def soft_ternary(grad_block, limit, peak_val, noise_val):
    clipped = jnp.clip(grad_block, -limit, limit)
    ratio = clipped / (peak_val + tiny_eps)
    value = jnp.clip(4.0 * ratio, -1.0, 1.0) * jnp.clip(
        2.0 * (jnp.abs(ratio) - noise_val.astype(jnp.float32)) + 0.5, 0.0, 1.0
    )
    return value.astype(jnp.bfloat16)


def adam_step(weight, moment, second, grad_val, decay, rate):
    moment_new = beta_one * moment + (1.0 - beta_one) * grad_val
    second_new = beta_two * second + (1.0 - beta_two) * grad_val * grad_val
    first_fix = 1.0 - beta_one**STEP
    second_fix = 1.0 - beta_two**STEP
    weight_new = weight - rate * (
        moment_new / first_fix / (jnp.sqrt(second_new / second_fix) + adam_eps) + decay * weight
    )
    return (weight_new, moment_new, second_new)


LONG_RING = 8


def spans_of(rows, count):
    marks = [rows * i // count // 16 * 16 for i in range(count)] + [rows]
    return list(zip(marks[:-1], marks[1:]))


def same(carried):
    return carried


def gather_whole(shard, group):
    return reorder(lax.all_gather(shard, "dp", axis=0), group)


def gather_queue(first, second, groups, near, hooks, carried):
    rings = lax.axis_size("dp") // 2
    rows = first.shape[0]
    middle = rows // 32 * 16
    sizes = [shard.shape[0] for shard in second]
    joined = jnp.concatenate(second)
    cut = joined.shape[0] - near
    ready = {
        ("a", 0): first[:middle],
        ("b", 0): first[middle:],
        ("f", 0): joined[:cut],
        ("n",): joined[cut:],
    }
    z_tasks = [(name, hop) for hop in range(rings - 1) for name in "ab"]
    z_tasks += [(name, hop) for hop in range(rings - 1) for name in "fp"]
    y_tasks = [(name, hop) for hop in range(rings) for name in "ab"]
    y_tasks += [("f", hop) for hop in range(rings)]

    def store(wholes, piece, step, flip, row):
        wholes = list(wholes)
        for spot, inner, count, outer in overlaps(sizes, row, piece.shape[0]):
            index = place(owner(step, flip), groups[1][spot])
            wholes[1 + spot] = put(wholes[1 + spot], piece[outer : outer + count], index, inner)
        return wholes

    def store_first(wholes, piece, step, flip, row):
        index = place(owner(step, flip), groups[0])
        return [put(wholes[0], piece, index, row)] + list(wholes[1:])

    wholes = None
    flight, pending, last = {}, None, {}
    step = 0
    while z_tasks or y_tasks or flight:
        started = {}
        if z_tasks and z_tasks[0] in ready:
            name, hop = z_tasks.pop(0)
            started["z", name, hop + 1] = turn(ready[name, hop])
        if y_tasks and y_tasks[0] in ready:
            name, hop = y_tasks.pop(0)
            started["y", name, hop] = swap(ready[name, hop], "dp", 1)
            if (name, hop) == ("b", rings - 2):
                started["y", "n", 0] = swap(ready["n",], "dp", 1)
        if step == 1:
            wholes = [jnp.zeros((2 * rings, *item.shape), item.dtype) for item in (first, *second)]
            wholes = store_first(wholes, ready["a", 0], 0, 0, 0)
            wholes = store_first(wholes, ready["b", 0], 0, 0, middle)
        if step == 2:
            wholes = store(wholes, ready["f", 0], 0, 0, 0)
            wholes = store(wholes, ready["n",], 0, 0, cut)
        later = None
        if step in hooks:
            carried, later = hooks[step](carried, wholes, last)
        flight, ready, wholes, carried, pending, last = settle(
            flight, ready, wholes, carried, pending, last
        )
        if pending is not None:
            carried = carried | pending
        pending = later
        for (axis, name, hop), piece in flight.items():
            if name in "ab":
                row = 0 if name == "a" else middle
                if axis == "y" and hop == rings - 1:
                    last[name] = piece
                else:
                    wholes = store_first(wholes, piece, hop, int(axis == "y"), row)
            elif name == "f":
                wholes = store(wholes, piece, hop, int(axis == "y"), 0)
                if axis == "y" and hop == rings - 1:
                    last[name] = piece
            elif name == "n":
                wholes = store(wholes, piece, 0, 1, cut)
                ready["p", 0] = jnp.concatenate([ready["n",], piece])
            else:
                if hop == rings - 1:
                    last[name] = piece
                for flip in (0, 1):
                    wholes = store(wholes, piece[flip * near : (flip + 1) * near], hop, flip, cut)
            if axis == "z":
                ready[name, hop] = piece
        flight = started
        step += 1
    return wholes, last, carried | (pending or {})


def scatter(grads, limits, tops, noises, groups, nears, ahead, beside, carried):
    rings = lax.axis_size("dp") // 2
    if rings > LONG_RING:
        for work in beside:
            carried = work(carried)
        results = []
        for grad, limit, top, noise, group in zip(grads, limits, tops, noises, groups):
            tern = soft_ternary(reorder(grad, group), limit, top, noise)
            total = lax.psum_scatter(tern.astype(jnp.float32), "dp", scatter_dimension=0)
            results.append(top * total)
        return results, carried
    beside = beside + [same] * (2 * rings - len(beside))
    spots = range(len(grads))
    cuts = [grad.shape[1] - near for grad, near in zip(grads, nears)]
    hops = rings - 1 if any(nears) else 1
    cutting = [
        spans_of(cut, hops) if near else [(0, cut)] + [None] * (hops - 1)
        for cut, near in zip(cuts, nears)
    ]

    ready = [
        soft_ternary(grad, limit, top, noise) if group is None else None
        for grad, limit, top, noise, group in zip(grads, limits, tops, noises, groups)
    ]

    def tern(spot, step, flip, row, count):
        index = owner(step, flip)
        if ready[spot] is not None:
            return take(ready[spot], index, row, count)
        return soft_ternary(
            take(grads[spot], place(index, groups[spot]), row, count),
            limits[spot],
            tops[spot],
            take(noises[spot], index, row, count),
        )

    def terns(step, flip, spans):
        return [
            None if span is None else tern(spot, step, flip, span[0], span[1] - span[0])
            for spot, span in zip(spots, spans)
        ]

    def far_terns(step, flip):
        return terns(step, flip, [(0, cut) for cut in cuts])

    def near_terns(step):
        return [
            jnp.concatenate([tern(spot, step, flip, cuts[spot], nears[spot]) for flip in (0, 1)])
            if nears[spot]
            else None
            for spot in spots
        ]

    def each(work, *lists):
        return [None if items[0] is None else work(*items) for items in zip(*lists)]

    def wide(value):
        return value.astype(jnp.float32)

    def narrow(value):
        return value.astype(jnp.bfloat16)

    def across(value):
        return swap(value, "dp", 1)

    order = list(range(1, rings)) + [0]
    pairs = near_terns(order[0])
    sending = [terns(order[0], 1, [cut[0] for cut in cutting])]
    limits, carried = settle(limits, carried)
    aways, owns = {}, {}
    got = [[] for spot in spots]
    for hop in range(1, hops + 1):
        others = each(across, sending[hop - 1])
        arrived = each(lambda item: turn(narrow(item)), pairs)
        more = near_terns(order[hop])
        if hop < hops:
            sending.append(terns(order[0], 1, [cut[hop] for cut in cutting]))
        if hop == 1:
            owns[0] = far_terns(order[0], 0)
        if hop == hops:
            aways[1] = far_terns(order[1], 1)
        carried = beside[hop - 1](carried)
        others, arrived, more, sending, aways, owns, limits, carried = settle(
            others, arrived, more, sending, aways, owns, limits, carried
        )
        pairs = each(lambda item, add: wide(item) + wide(add), arrived, more)
        for spot in spots:
            if others[spot] is not None:
                got[spot].append(others[spot])
    sums = [wide(owns[0][spot]) + wide(jnp.concatenate(got[spot])) for spot in spots]
    for spin in range(1, rings):
        others = each(across, aways[spin])
        moved = each(lambda item: turn(narrow(item)), sums)
        lasts = None
        if spin == rings - 1:
            lasts = [
                item if item is None else across(narrow(item[near:]))
                for item, near in zip(pairs, nears)
            ]
        for later in range(spin, rings if ahead else spin + 1):
            if later not in owns:
                owns[later] = far_terns(order[later], 0)
        for later in range(spin + 1, rings if ahead else min(spin + 2, rings)):
            if later not in aways:
                aways[later] = far_terns(order[later], 1)
        carried = beside[hops - 1 + spin](carried)
        others, moved, lasts, pairs, aways, owns, limits, carried = settle(
            others, moved, lasts, pairs, aways, owns, limits, carried
        )
        sums = each(
            lambda own, item, more: wide(own) + wide(item) + wide(more), owns[spin], others, moved
        )
    results = []
    for spot, near in zip(spots, nears):
        total = sums[spot]
        if near:
            total = jnp.concatenate([total, pairs[spot][:near] + wide(lasts[spot])])
        results.append(tops[spot] * total)
    return results, carried


def shards(
    features,
    labels,
    noise_six,
    noise_seven,
    noise_eight,
    w_six,
    w_seven,
    w_eight,
    m_six,
    m_seven,
    m_eight,
    v_six,
    v_seven,
    v_eight,
    biases,
    bias_out,
    m_biases,
    v_biases,
    m_bias_out,
    v_bias_out,
):
    mine = lax.axis_index("mp")
    replicas = lax.axis_size("dp")
    ways = lax.axis_size("mp")
    rings = replicas // 2
    batch_rows = features.shape[0]
    tokens = batch_rows * replicas
    half = batch_rows // 2
    width = biases.shape[1]
    outs = bias_out.shape[0]
    padded = outs + -outs % 128
    rows_six, rows_seven, rows_eight = w_six.shape[0], w_seven.shape[0], w_eight.shape[0]
    group_six, group_seven = features.shape[1] // rows_six, width // rows_seven
    near_six = near_rows(rows_six, rings)
    bits = list(reversed(list(spread_bits("mp"))))
    far_bits, near_bit = bits[:-1], bits[-1]

    def widen(value):
        return jnp.pad(value, ((0, 0), (0, padded - outs)))

    def halves(value):
        return [value[:half], value[half:]]

    def over_far(own):
        done = xor_blocks(own, far_bits)
        del done[0]
        return done

    def over_near(blocks):
        return {step ^ near_bit: swap(item, "mp", near_bit) for step, item in blocks.items()}

    def join(halves_of_blocks):
        return jnp.concatenate(
            [
                jnp.concatenate([blocks[step] for step in range(ways)], axis=1)
                for blocks in halves_of_blocks
            ]
        )

    far_features = over_far(features)
    shards_cast = [
        w_six.astype(jnp.bfloat16),
        widen(w_eight.astype(jnp.bfloat16)),
        w_seven.astype(jnp.bfloat16),
    ]
    if rings > LONG_RING:
        inputs = join([{0: features} | far_features | over_near({0: features} | far_features)])
        noise_wide = widen(noise_eight)
        kept_six = gather_whole(shards_cast[0], group_six).reshape(-1, width)
        kept_eight = gather_whole(shards_cast[1], None)
        kept_seven = gather_whole(shards_cast[2], group_seven)
        pre_six, out_six = layer_forward(matmul(inputs, kept_six), biases[0])
        hidden_blocks = []
        for item in halves(out_six):
            blocks = {0: item} | over_far(item)
            hidden_blocks.append(blocks | over_near(blocks))
        hiddens = [join([blocks]) for blocks in hidden_blocks]

        def sum_seven(number):
            return matmul(hiddens[number], kept_seven.reshape(-1, width))

    else:
        count = 2 * rings

        def own_near(carried, wholes, last):
            return {"near": swap(features, "mp", near_bit), "noise": widen(noise_eight)}, None

        def far_there(carried, wholes, last):
            return carried | {"far": far_features}, None

        def far_near(carried, wholes, last):
            return carried | {"both": over_near(carried["far"])}, None

        def join_inputs(carried, wholes, last):
            blocks = {0: features, near_bit: carried["near"]} | carried["far"] | carried["both"]
            return {"inputs": join([blocks]), "noise": carried["noise"]}, None

        def fc_six_most(carried, wholes, last):
            early = matmul(carried["inputs"], wholes[0].reshape(-1, width))
            return carried, {"early": early}

        def fc_six_rest(carried, wholes, last):
            start = place(owner(rings - 1, 1), group_six) * rows_six
            columns = lax.dynamic_slice_in_dim(carried["inputs"], start, rows_six, 1)
            rest = matmul(columns, jnp.concatenate([last["a"], last["b"]]))
            pre_six, out_six = layer_forward(carried["early"] + rest, biases[0])
            one, two = halves(out_six)
            crossing["one"], crossing["two"] = over_far(one), over_far(two)
            return (
                {"inputs": carried["inputs"], "noise": carried["noise"], "pre": pre_six, "out": (one, two)},
                None,
            )

        crossing = {}

        def hidden_own(carried, wholes, last):
            own = [over_near({0: item}) for item in carried["out"]]
            return carried | {"own": own}, None

        def hidden_one(carried, wholes, last):
            return carried | {"one": crossing["one"]}, None

        def hidden_one_near(carried, wholes, last):
            blocks = {0: carried["out"][0]} | carried["own"][0] | carried["one"]
            hidden = join([blocks | over_near(carried["one"])])
            early = matmul(hidden, wholes[2].reshape(-1, width))
            return carried, {"hidden_one": hidden, "early_one": early}

        def fc_seven_most(carried, wholes, last):
            far = crossing["two"]
            two = join([{0: carried["out"][1]} | carried["own"][1] | far | over_near(far)])
            names = ("inputs", "noise", "pre")
            return {name: carried[name] for name in names} | {"hidden_two": two}, None

        hooks = {
            1: own_near,
            count - 4: far_there,
            count - 3: far_near,
            count - 2: join_inputs,
            count - 1: fc_six_most,
            count + 1: fc_six_rest,
            count + 2: hidden_own,
            count + 3: hidden_one,
            count + 4: hidden_one_near,
            count + 5: fc_seven_most,
        }
        near = (rows_six + rows_seven + rows_eight) // (2 * rings - 2) // 16 * 16
        (_, kept_eight, kept_seven), last, carried = gather_queue(
            shards_cast[0],
            shards_cast[1:],
            [group_six, [None, group_seven]],
            min(near, rows_seven // 32 * 16),
            hooks,
            {},
        )
        inputs, noise_wide, pre_six = carried["inputs"], carried["noise"], carried["pre"]
        hiddens = [carried["hidden_one"], carried["hidden_two"]]
        start = place(owner(rings - 1, 1), group_seven) * rows_seven
        other_start = place(owner(rings - 1, 0), group_seven) * rows_seven
        rest = last["f"][rows_eight:]
        count, most = last["p"].shape[0] // 2, rest.shape[0]

        def columns(number, low, size):
            return lax.dynamic_slice_in_dim(hiddens[number], low, size, 1)

        def sum_seven(number):
            if number == 1:
                return matmul(hiddens[1], kept_seven)
            whole_block = jnp.concatenate([rest, last["p"][count:]])
            return (
                carried["early_one"]
                + matmul(columns(0, start, rows_seven), whole_block)
                + matmul(columns(0, other_start + most, count), last["p"][:count])
            )

    kept_seven, kept_eight = kept_seven.reshape(-1, width), kept_eight.reshape(-1, padded)

    bias_wide = jnp.pad(bias_out, (0, padded - outs), constant_values=-1e30)
    share = half // ways

    def half_forward(number, earlier):
        pre, out = layer_forward(sum_seven(number), biases[1])
        if earlier is not None:
            pre, out, earlier = settle(pre, out, earlier)
        shares = out.reshape(ways, share, width)
        parts = {
            step: matmul(lax.dynamic_index_in_dim(shares, mine ^ step, 0, keepdims=False), kept_eight)
            for step in range(ways)
        }
        for bit in reversed(bits):
            for step in range(0, ways, 2 * bit):
                parts[step] = parts[step] + swap(parts[step + bit], "mp", bit)
        logits = parts[0] + bias_wide
        labels_part = lax.dynamic_slice_in_dim(labels, number * half + mine * share, share, 0)
        top_logit = jnp.max(logits, axis=1, keepdims=True)
        shifted = jnp.exp(logits - top_logit)
        row_total = jnp.sum(shifted, axis=1, keepdims=True)
        log_total = top_logit[:, 0] + jnp.log(row_total[:, 0])
        classes = lax.broadcasted_iota(jnp.int32, logits.shape, 1)
        onehot = (classes == labels_part[:, None]).astype(jnp.float32)
        loss_part = jnp.sum(log_total - jnp.sum(onehot * logits, axis=1)) / tokens
        dz_part = ((shifted / row_total - onehot) / tokens).astype(jnp.bfloat16)
        dlogits = jnp.zeros((ways, share, padded), jnp.bfloat16)
        for step, item in xor_blocks(dz_part, bits).items():
            dlogits = put(dlogits, item, mine ^ step)
        return pre, out, dlogits.reshape(half, padded), loss_part, logits

    both = [half_forward(0, None)]
    both.append(half_forward(1, both[0][4]))
    dlogits = jnp.concatenate([item[2] for item in both])
    pre_seven, out_seven, _ = settle(
        [item[0] for item in both], [item[1] for item in both], both[0][4][:8, :128]
    )
    pre_seven, out_seven = jnp.concatenate(pre_seven), jnp.concatenate(out_seven)
    pre_seven, out_seven, dlogits = settle(pre_seven, out_seven, dlogits)
    loss_part = both[0][3] + both[1][3]
    hidden = jnp.concatenate(hiddens)

    delta_seven = layer_delta(pre_seven, against_rows(dlogits, kept_eight))

    def upstream(delta, step):
        return against_rows(delta, kept_seven[step * width : (step + 1) * width])

    top_bit = bits[0]
    cuts = [0] + [batch_rows // 64 * mark for mark in (8, 27, 46)] + [batch_rows]

    def near_sums(first, delta):
        ups = {step: upstream(delta, step) for step in range(first, first + top_bit)}
        for bit in reversed(bits[1:]):
            for step in range(first, first + top_bit, 2 * bit):
                ups[step] = ups[step] + swap(ups[step + bit], "mp", bit)
        return ups[first]

    crossing = near_sums(top_bit, delta_seven)
    grad_eight = contract_rows(out_seven, dlogits)
    limit_eight, peak_eight = grad_limits(grad_eight, outs)
    crossing, grad_eight, limit_eight, peak_eight, delta_seven, dlogits = settle(
        crossing, grad_eight, limit_eight, peak_eight, delta_seven, dlogits
    )
    crossing = [crossing[low:high] for low, high in zip(cuts[:-1], cuts[1:])]
    crossed = [swap(crossing[0], "mp", top_bit)]
    grad_seven = contract_rows(hidden, delta_seven)
    limit_seven, peak_seven = grad_limits(grad_seven, width)
    tops = fold(jnp.stack([peak_eight, peak_seven]), jnp.maximum, ("dp",))
    crossing, crossed, grad_seven, limit_seven, tops, delta_seven = settle(
        crossing, crossed, grad_seven, limit_seven, tops, delta_seven
    )
    top_eight, top_seven = tops[0], tops[1]

    def cross(step):
        def work(carried):
            delta, crossing, crossed, own_up = carried
            if step == 0:
                own_up = near_sums(0, delta)
            return (delta, crossing, crossed + [swap(crossing[step + 1], "mp", top_bit)], own_up)

        return work

    def grad_fc_six(carried):
        _, _, crossed, own_up = carried
        delta_six = layer_delta(pre_six, own_up + jnp.concatenate(crossed))
        grad_six = contract_rows(inputs, delta_six)
        limit_six, peak_six = grad_limits(grad_six, width)
        return (delta_six, grad_six, limit_six, peak_six)

    def sum_or_max(one, two):
        return jnp.concatenate([one[:-1] + two[:-1], jnp.maximum(one[-1:], two[-1:])])

    def small_sums(carried):
        delta_six, grad_six, limit_six, peak_six = carried
        columns = [
            jnp.sum(item.astype(jnp.float32), axis=0) for item in (delta_six, delta_seven, dlogits)
        ]
        small = fold(jnp.concatenate(columns + [peak_six[None]]), sum_or_max, ("dp",))
        return (grad_six, limit_six, small)

    beside = [
        cross(0),
        cross(1),
        cross(2),
        grad_fc_six,
    ]
    (reduced_eight, reduced_seven), carried = scatter(
        [grad_eight.reshape(replicas, rows_eight, padded), grad_seven.reshape(replicas, rows_seven, width)],
        [limit_eight, limit_seven],
        [top_eight, top_seven],
        [noise_wide.reshape(replicas, rows_eight, padded), noise_seven.reshape(replicas, rows_seven, width)],
        [None, group_seven],
        [0, 0],
        False,
        beside,
        (delta_seven, crossing, crossed, None),
    )
    grad_six, limit_six, small = small_sums(carried)
    top_six = small[-1]
    (reduced_six,), (reduced_seven, reduced_eight) = scatter(
        [grad_six.reshape(replicas, rows_six, width)],
        [limit_six],
        [top_six],
        [noise_six.reshape(replicas, rows_six, width)],
        [group_six],
        [near_six],
        False,
        [same] * rings + [lambda carried: (carried[0], carried[1].T)],
        (reduced_seven, reduced_eight[:, :outs]),
    )
    grad_pair = small[: 2 * width].reshape(2, width)
    grad_out = small[2 * width : 2 * width + outs]
    squares = (
        jnp.sum(reduced_six * reduced_six)
        + jnp.sum(reduced_seven * reduced_seven)
        + jnp.sum(reduced_eight * reduced_eight)
        + jnp.sum(grad_pair * grad_pair) / replicas
        + jnp.sum(grad_out * grad_out) / (replicas * ways)
    )
    totals = fold(jnp.stack([squares, loss_part]), jnp.add, ("dp", "mp"))
    total_squares, loss = totals[0], totals[1]
    grad_norm = jnp.sqrt(total_squares)
    factor = clip_norm / jnp.maximum(grad_norm, clip_norm)
    new_six, new_m_six, new_v_six = adam_step(
        w_six, m_six, v_six, factor * reduced_six, decay_rate, learn_rate
    )
    new_seven, new_m_seven, new_v_seven = adam_step(
        w_seven, m_seven, v_seven, factor * reduced_seven, decay_rate, learn_rate
    )
    new_eight, new_m_eight, new_v_eight = (
        item.T
        for item in adam_step(
            w_eight.T, m_eight.T, v_eight.T, factor * reduced_eight, decay_rate, learn_rate
        )
    )
    new_biases, new_m_biases, new_v_biases = adam_step(
        biases, m_biases, v_biases, factor * grad_pair, 0.0, bias_rate
    )
    new_bias_out, new_m_bias_out, new_v_bias_out = adam_step(
        bias_out, m_bias_out, v_bias_out, factor * grad_out, 0.0, bias_rate
    )
    return (
        loss,
        grad_norm,
        new_six,
        new_seven,
        new_eight,
        new_m_six,
        new_m_seven,
        new_m_eight,
        new_v_six,
        new_v_seven,
        new_v_eight,
        new_six.astype(jnp.bfloat16),
        new_seven.astype(jnp.bfloat16),
        new_eight.astype(jnp.bfloat16),
        new_biases,
        new_bias_out,
        new_m_biases,
        new_v_biases,
        new_m_bias_out,
        new_v_bias_out,
    )


def solution(mesh):
    return jax.shard_map(
        shards,
        mesh=mesh,
        in_specs=(
            P("dp", "mp"),
            P("dp"),
            P("dp", "mp"),
            P("dp", "mp"),
            P(("dp", "mp"), None),
            P("dp", "mp"),
            P("dp", "mp"),
            P(("mp", "dp"), None),
            P("dp", "mp"),
            P("dp", "mp"),
            P(("mp", "dp"), None),
            P("dp", "mp"),
            P("dp", "mp"),
            P(("mp", "dp"), None),
            P(None, "mp"),
            P(),
            P(None, "mp"),
            P(None, "mp"),
            P(),
            P(),
        ),
        out_specs=(
            P(),
            P(),
            P("dp", "mp"),
            P("dp", "mp"),
            P(("mp", "dp"), None),
            P("dp", "mp"),
            P("dp", "mp"),
            P(("mp", "dp"), None),
            P("dp", "mp"),
            P("dp", "mp"),
            P(("mp", "dp"), None),
            P("dp", "mp"),
            P("dp", "mp"),
            P(("mp", "dp"), None),
            P(None, "mp"),
            P(),
            P(None, "mp"),
            P(None, "mp"),
            P(),
            P(),
        ),
        check_vma=False,
    )
```

```python
import jax
import jax.numpy as jnp
from jax import lax
from jax.sharding import PartitionSpec as P

STEP = 3


beta_one = 0.5
beta_two = 0.5
learn_rate = 0.01
bias_rate = 0.05
decay_rate = 0.1
adam_eps = 1e-08
clip_norm = 0.05
tiny_eps = 1e-12


def matmul(left, right):
    return jnp.dot(left, right, preferred_element_type=jnp.float32)


def contract_rows(left, right):
    return lax.dot_general(
        left, right, (((0,), (0,)), ((), ())), preferred_element_type=jnp.float32
    )


def against_rows(left, right):
    return lax.dot_general(
        left, right, (((1,), (1,)), ((), ())), preferred_element_type=jnp.float32
    )


def layer_forward(pre_sum, bias_row):
    pre_act = pre_sum + bias_row
    return (pre_act, jax.nn.silu(pre_act).astype(jnp.bfloat16))


def layer_delta(pre_act, upstream):
    sigmoid_val = jax.nn.sigmoid(pre_act)
    slope = sigmoid_val * (1.0 + pre_act * (1.0 - sigmoid_val))
    return (upstream * slope).astype(jnp.bfloat16)


def grad_limits(grad_block, columns):
    squares = jnp.sum(grad_block * grad_block)
    limit = 2.5 * jnp.sqrt(squares / (grad_block.shape[0] * columns))
    return (limit, jnp.minimum(jnp.max(jnp.abs(grad_block)), limit))


def swap(value, axis, bit):
    size = lax.axis_size(axis)
    return lax.ppermute(value, axis, [(i, i ^ bit) for i in range(size)])


def turn(value):
    size = lax.axis_size("dp")
    return lax.ppermute(value, "dp", [(i, (i + 2) % size) for i in range(size)])


def spread_bits(axis):
    bit = 1
    while bit < lax.axis_size(axis):
        yield bit
        bit *= 2


def fold(value, combine, axes):
    for axis in axes:
        for bit in spread_bits(axis):
            value = combine(value, swap(value, axis, bit))
    return value


def settle(*values):
    return lax.optimization_barrier(values)


def owner(step, flip):
    size = lax.axis_size("dp")
    here = lax.axis_index("dp")
    return ((here + size - 2 * step) % size) ^ flip


def place(index, blocks):
    if blocks is None:
        return index
    mine = lax.axis_index("mp")
    return ((index // blocks) ^ mine) * blocks + index % blocks


def put(whole, piece, index, row=0):
    return lax.dynamic_update_slice(whole, piece[None], (index, row, 0))


def take(whole, index, row, rows):
    return lax.dynamic_slice(whole, (index, row, 0), (1, rows, whole.shape[2]))[0]


def xor_blocks(value, bits):
    blocks = {0: value}
    for bit in bits:
        blocks |= {step ^ bit: swap(item, "mp", bit) for step, item in blocks.items()}
    return blocks


def near_rows(rows, rings):
    return max(16, (rows // (2 * rings + 2) + 8) // 16 * 16)


def reorder(whole, group):
    if group is None:
        return whole
    mine = lax.axis_index("mp")
    ways = whole.shape[0] // group
    grouped = whole.reshape(ways, group, *whole.shape[1:])
    return jnp.concatenate(
        [lax.dynamic_index_in_dim(grouped, mine ^ step, 0, keepdims=False) for step in range(ways)]
    )


def overlaps(sizes, row, count):
    start = 0
    for spot, size in enumerate(sizes):
        low, high = max(row, start), min(row + count, start + size)
        if low < high:
            yield spot, low - start, high - low, low - row
        start += size


def soft_ternary(grad_block, limit, peak_val, noise_val):
    clipped = jnp.clip(grad_block, -limit, limit)
    ratio = clipped / (peak_val + tiny_eps)
    value = jnp.clip(4.0 * ratio, -1.0, 1.0) * jnp.clip(
        2.0 * (jnp.abs(ratio) - noise_val.astype(jnp.float32)) + 0.5, 0.0, 1.0
    )
    return value.astype(jnp.bfloat16)


def adam_step(weight, moment, second, grad_val, decay, rate):
    moment_new = beta_one * moment + (1.0 - beta_one) * grad_val
    second_new = beta_two * second + (1.0 - beta_two) * grad_val * grad_val
    first_fix = 1.0 - beta_one**STEP
    second_fix = 1.0 - beta_two**STEP
    weight_new = weight - rate * (
        moment_new / first_fix / (jnp.sqrt(second_new / second_fix) + adam_eps) + decay * weight
    )
    return (weight_new, moment_new, second_new)


LONG_RING = 8


def spans_of(rows, count):
    marks = [rows * i // count // 16 * 16 for i in range(count)] + [rows]
    return list(zip(marks[:-1], marks[1:]))


def same(carried):
    return carried


def gather_whole(shard, group):
    return reorder(lax.all_gather(shard, "dp", axis=0), group)


def gather_queue(first, second, groups, near, hooks, carried):
    rings = lax.axis_size("dp") // 2
    rows = first.shape[0]
    middle = rows // 32 * 16
    sizes = [shard.shape[0] for shard in second]
    joined = jnp.concatenate(second)
    cut = joined.shape[0] - near
    ready = {
        ("a", 0): first[:middle],
        ("b", 0): first[middle:],
        ("f", 0): joined[:cut],
        ("n",): joined[cut:],
    }
    z_tasks = [(name, hop) for hop in range(rings - 1) for name in "ab"]
    z_tasks += [(name, hop) for hop in range(rings - 1) for name in "fp"]
    y_tasks = [(name, hop) for hop in range(rings) for name in "ab"]
    y_tasks += [("f", hop) for hop in range(rings)]

    def store(wholes, piece, step, flip, row):
        wholes = list(wholes)
        for spot, inner, count, outer in overlaps(sizes, row, piece.shape[0]):
            index = place(owner(step, flip), groups[1][spot])
            wholes[1 + spot] = put(wholes[1 + spot], piece[outer : outer + count], index, inner)
        return wholes

    def store_first(wholes, piece, step, flip, row):
        index = place(owner(step, flip), groups[0])
        return [put(wholes[0], piece, index, row)] + list(wholes[1:])

    wholes = None
    flight, pending, last = {}, None, {}
    step = 0
    while z_tasks or y_tasks or flight:
        started = {}
        if z_tasks and z_tasks[0] in ready:
            name, hop = z_tasks.pop(0)
            started["z", name, hop + 1] = turn(ready[name, hop])
        if y_tasks and y_tasks[0] in ready:
            name, hop = y_tasks.pop(0)
            started["y", name, hop] = swap(ready[name, hop], "dp", 1)
            if (name, hop) == ("b", rings - 2):
                started["y", "n", 0] = swap(ready["n",], "dp", 1)
        if step == 1:
            wholes = [jnp.zeros((2 * rings, *item.shape), item.dtype) for item in (first, *second)]
            wholes = store_first(wholes, ready["a", 0], 0, 0, 0)
            wholes = store_first(wholes, ready["b", 0], 0, 0, middle)
        if step == 2:
            wholes = store(wholes, ready["f", 0], 0, 0, 0)
            wholes = store(wholes, ready["n",], 0, 0, cut)
        later = None
        if step in hooks:
            carried, later = hooks[step](carried, wholes, last)
        flight, ready, wholes, carried, pending, last = settle(
            flight, ready, wholes, carried, pending, last
        )
        if pending is not None:
            carried = carried | pending
        pending = later
        for (axis, name, hop), piece in flight.items():
            if name in "ab":
                row = 0 if name == "a" else middle
                if axis == "y" and hop == rings - 1:
                    last[name] = piece
                else:
                    wholes = store_first(wholes, piece, hop, int(axis == "y"), row)
            elif name == "f":
                wholes = store(wholes, piece, hop, int(axis == "y"), 0)
                if axis == "y" and hop == rings - 1:
                    last[name] = piece
            elif name == "n":
                wholes = store(wholes, piece, 0, 1, cut)
                ready["p", 0] = jnp.concatenate([ready["n",], piece])
            else:
                if hop == rings - 1:
                    last[name] = piece
                for flip in (0, 1):
                    wholes = store(wholes, piece[flip * near : (flip + 1) * near], hop, flip, cut)
            if axis == "z":
                ready[name, hop] = piece
        flight = started
        step += 1
    return wholes, last, carried | (pending or {})


def scatter(grads, limits, tops, noises, groups, nears, ahead, beside, carried):
    rings = lax.axis_size("dp") // 2
    if rings > LONG_RING:
        for work in beside:
            carried = work(carried)
        results = []
        for grad, limit, top, noise, group in zip(grads, limits, tops, noises, groups):
            tern = soft_ternary(reorder(grad, group), limit, top, noise)
            total = lax.psum_scatter(tern.astype(jnp.float32), "dp", scatter_dimension=0)
            results.append(top * total)
        return results, carried
    beside = beside + [same] * (2 * rings - len(beside))
    spots = range(len(grads))
    cuts = [grad.shape[1] - near for grad, near in zip(grads, nears)]
    hops = rings - 1 if any(nears) else 1
    cutting = [
        spans_of(cut, hops) if near else [(0, cut)] + [None] * (hops - 1)
        for cut, near in zip(cuts, nears)
    ]

    ready = [
        soft_ternary(grad, limit, top, noise) if group is None else None
        for grad, limit, top, noise, group in zip(grads, limits, tops, noises, groups)
    ]

    def tern(spot, step, flip, row, count):
        index = owner(step, flip)
        if ready[spot] is not None:
            return take(ready[spot], index, row, count)
        return soft_ternary(
            take(grads[spot], place(index, groups[spot]), row, count),
            limits[spot],
            tops[spot],
            take(noises[spot], index, row, count),
        )

    def terns(step, flip, spans):
        return [
            None if span is None else tern(spot, step, flip, span[0], span[1] - span[0])
            for spot, span in zip(spots, spans)
        ]

    def far_terns(step, flip):
        return terns(step, flip, [(0, cut) for cut in cuts])

    def near_terns(step):
        return [
            jnp.concatenate([tern(spot, step, flip, cuts[spot], nears[spot]) for flip in (0, 1)])
            if nears[spot]
            else None
            for spot in spots
        ]

    def each(work, *lists):
        return [None if items[0] is None else work(*items) for items in zip(*lists)]

    def wide(value):
        return value.astype(jnp.float32)

    def narrow(value):
        return value.astype(jnp.bfloat16)

    def across(value):
        return swap(value, "dp", 1)

    order = list(range(1, rings)) + [0]
    pairs = near_terns(order[0])
    sending = [terns(order[0], 1, [cut[0] for cut in cutting])]
    limits, carried = settle(limits, carried)
    aways, owns = {}, {}
    got = [[] for spot in spots]
    for hop in range(1, hops + 1):
        others = each(across, sending[hop - 1])
        arrived = each(lambda item: turn(narrow(item)), pairs)
        more = near_terns(order[hop])
        if hop < hops:
            sending.append(terns(order[0], 1, [cut[hop] for cut in cutting]))
        if hop == 1:
            owns[0] = far_terns(order[0], 0)
        if hop == hops:
            aways[1] = far_terns(order[1], 1)
        carried = beside[hop - 1](carried)
        others, arrived, more, sending, aways, owns, limits, carried = settle(
            others, arrived, more, sending, aways, owns, limits, carried
        )
        pairs = each(lambda item, add: wide(item) + wide(add), arrived, more)
        for spot in spots:
            if others[spot] is not None:
                got[spot].append(others[spot])
    sums = [wide(owns[0][spot]) + wide(jnp.concatenate(got[spot])) for spot in spots]
    for spin in range(1, rings):
        others = each(across, aways[spin])
        moved = each(lambda item: turn(narrow(item)), sums)
        lasts = None
        if spin == rings - 1:
            lasts = [
                item if item is None else across(narrow(item[near:]))
                for item, near in zip(pairs, nears)
            ]
        for later in range(spin, rings if ahead else spin + 1):
            if later not in owns:
                owns[later] = far_terns(order[later], 0)
        for later in range(spin + 1, rings if ahead else min(spin + 2, rings)):
            if later not in aways:
                aways[later] = far_terns(order[later], 1)
        carried = beside[hops - 1 + spin](carried)
        others, moved, lasts, pairs, aways, owns, limits, carried = settle(
            others, moved, lasts, pairs, aways, owns, limits, carried
        )
        sums = each(
            lambda own, item, more: wide(own) + wide(item) + wide(more), owns[spin], others, moved
        )
    results = []
    for spot, near in zip(spots, nears):
        total = sums[spot]
        if near:
            total = jnp.concatenate([total, pairs[spot][:near] + wide(lasts[spot])])
        results.append(tops[spot] * total)
    return results, carried


def shards(
    features,
    labels,
    noise_six,
    noise_seven,
    noise_eight,
    w_six,
    w_seven,
    w_eight,
    m_six,
    m_seven,
    m_eight,
    v_six,
    v_seven,
    v_eight,
    biases,
    bias_out,
    m_biases,
    v_biases,
    m_bias_out,
    v_bias_out,
):
    mine = lax.axis_index("mp")
    replicas = lax.axis_size("dp")
    ways = lax.axis_size("mp")
    rings = replicas // 2
    batch_rows = features.shape[0]
    tokens = batch_rows * replicas
    half = batch_rows // 2
    width = biases.shape[1]
    outs = bias_out.shape[0]
    padded = outs + -outs % 128
    rows_six, rows_seven, rows_eight = w_six.shape[0], w_seven.shape[0], w_eight.shape[0]
    group_six, group_seven = features.shape[1] // rows_six, width // rows_seven
    near_six = max(16, near_rows(rows_six, rings) - 16)
    bits = list(reversed(list(spread_bits("mp"))))
    far_bits, near_bit = bits[:-1], bits[-1]

    def widen(value):
        return jnp.pad(value, ((0, 0), (0, padded - outs)))

    def halves(value):
        return [value[:half], value[half:]]

    def over_far(own):
        done = xor_blocks(own, far_bits)
        del done[0]
        return done

    def over_near(blocks):
        return {step ^ near_bit: swap(item, "mp", near_bit) for step, item in blocks.items()}

    def join(halves_of_blocks):
        return jnp.concatenate(
            [
                jnp.concatenate([blocks[step] for step in range(ways)], axis=1)
                for blocks in halves_of_blocks
            ]
        )

    far_features = over_far(features)
    shards_cast = [
        w_six.astype(jnp.bfloat16),
        widen(w_eight.astype(jnp.bfloat16)),
        w_seven.astype(jnp.bfloat16),
    ]
    if rings > LONG_RING:
        inputs = join([{0: features} | far_features | over_near({0: features} | far_features)])
        noise_wide = widen(noise_eight)
        kept_six = gather_whole(shards_cast[0], group_six).reshape(-1, width)
        kept_eight = gather_whole(shards_cast[1], None)
        kept_seven = gather_whole(shards_cast[2], group_seven)
        pre_six, out_six = layer_forward(matmul(inputs, kept_six), biases[0])
        hidden_blocks = []
        for item in halves(out_six):
            blocks = {0: item} | over_far(item)
            hidden_blocks.append(blocks | over_near(blocks))
        hiddens = [join([blocks]) for blocks in hidden_blocks]

        def sum_seven(number):
            return matmul(hiddens[number], kept_seven.reshape(-1, width))

    else:
        count = 2 * rings

        def own_near(carried, wholes, last):
            return {"near": swap(features, "mp", near_bit), "noise": widen(noise_eight)}, None

        def far_there(carried, wholes, last):
            return carried | {"far": far_features}, None

        def far_near(carried, wholes, last):
            return carried | {"both": over_near(carried["far"])}, None

        def join_inputs(carried, wholes, last):
            blocks = {0: features, near_bit: carried["near"]} | carried["far"] | carried["both"]
            return {"inputs": join([blocks]), "noise": carried["noise"]}, None

        def fc_six_most(carried, wholes, last):
            early = matmul(carried["inputs"], wholes[0].reshape(-1, width))
            return carried, {"early": early}

        def fc_six_rest(carried, wholes, last):
            start = place(owner(rings - 1, 1), group_six) * rows_six
            columns = lax.dynamic_slice_in_dim(carried["inputs"], start, rows_six, 1)
            rest = matmul(columns, jnp.concatenate([last["a"], last["b"]]))
            pre_six, out_six = layer_forward(carried["early"] + rest, biases[0])
            one, two = halves(out_six)
            crossing["one"], crossing["two"] = over_far(one), over_far(two)
            return (
                {"inputs": carried["inputs"], "noise": carried["noise"], "pre": pre_six, "out": (one, two)},
                None,
            )

        crossing = {}

        def hidden_own(carried, wholes, last):
            own = [over_near({0: item}) for item in carried["out"]]
            return carried | {"own": own}, None

        def hidden_one(carried, wholes, last):
            return carried | {"one": crossing["one"]}, None

        def hidden_one_near(carried, wholes, last):
            blocks = {0: carried["out"][0]} | carried["own"][0] | carried["one"]
            hidden = join([blocks | over_near(carried["one"])])
            early = matmul(hidden, wholes[2].reshape(-1, width))
            return carried, {"hidden_one": hidden, "early_one": early}

        def fc_seven_most(carried, wholes, last):
            far = crossing["two"]
            two = join([{0: carried["out"][1]} | carried["own"][1] | far | over_near(far)])
            names = ("inputs", "noise", "pre")
            return {name: carried[name] for name in names} | {"hidden_two": two}, None

        hooks = {
            1: own_near,
            count - 4: far_there,
            count - 3: far_near,
            count - 2: join_inputs,
            count - 1: fc_six_most,
            count + 1: fc_six_rest,
            count + 2: hidden_own,
            count + 3: hidden_one,
            count + 4: hidden_one_near,
            count + 5: fc_seven_most,
        }
        near = (rows_six + rows_seven + rows_eight) // (2 * rings - 2) // 16 * 16
        (_, kept_eight, kept_seven), last, carried = gather_queue(
            shards_cast[0],
            shards_cast[1:],
            [group_six, [None, group_seven]],
            min(near, rows_seven // 32 * 16),
            hooks,
            {},
        )
        inputs, noise_wide, pre_six = carried["inputs"], carried["noise"], carried["pre"]
        hiddens = [carried["hidden_one"], carried["hidden_two"]]
        start = place(owner(rings - 1, 1), group_seven) * rows_seven
        other_start = place(owner(rings - 1, 0), group_seven) * rows_seven
        rest = last["f"][rows_eight:]
        count, most = last["p"].shape[0] // 2, rest.shape[0]

        def columns(number, low, size):
            return lax.dynamic_slice_in_dim(hiddens[number], low, size, 1)

        def sum_seven(number):
            if number == 1:
                return matmul(hiddens[1], kept_seven)
            whole_block = jnp.concatenate([rest, last["p"][count:]])
            return (
                carried["early_one"]
                + matmul(columns(0, start, rows_seven), whole_block)
                + matmul(columns(0, other_start + most, count), last["p"][:count])
            )

    kept_seven, kept_eight = kept_seven.reshape(-1, width), kept_eight.reshape(-1, padded)

    bias_wide = jnp.pad(bias_out, (0, padded - outs), constant_values=-1e30)
    share = half // ways

    def half_forward(number, earlier):
        pre, out = layer_forward(sum_seven(number), biases[1])
        if earlier is not None:
            pre, out, earlier = settle(pre, out, earlier)
        shares = out.reshape(ways, share, width)
        parts = {
            step: matmul(lax.dynamic_index_in_dim(shares, mine ^ step, 0, keepdims=False), kept_eight)
            for step in range(ways)
        }
        for bit in reversed(bits):
            for step in range(0, ways, 2 * bit):
                parts[step] = parts[step] + swap(parts[step + bit], "mp", bit)
        logits = parts[0] + bias_wide
        labels_part = lax.dynamic_slice_in_dim(labels, number * half + mine * share, share, 0)
        top_logit = jnp.max(logits, axis=1, keepdims=True)
        shifted = jnp.exp(logits - top_logit)
        row_total = jnp.sum(shifted, axis=1, keepdims=True)
        log_total = top_logit[:, 0] + jnp.log(row_total[:, 0])
        classes = lax.broadcasted_iota(jnp.int32, logits.shape, 1)
        onehot = (classes == labels_part[:, None]).astype(jnp.float32)
        loss_part = jnp.sum(log_total - jnp.sum(onehot * logits, axis=1)) / tokens
        dz_part = ((shifted / row_total - onehot) / tokens).astype(jnp.bfloat16)
        dlogits = jnp.zeros((ways, share, padded), jnp.bfloat16)
        for step, item in xor_blocks(dz_part, bits).items():
            dlogits = put(dlogits, item, mine ^ step)
        return pre, out, dlogits.reshape(half, padded), loss_part, logits

    both = [half_forward(0, None)]
    both.append(half_forward(1, both[0][4]))
    dlogits = jnp.concatenate([item[2] for item in both])
    pre_seven, out_seven, _ = settle(
        [item[0] for item in both], [item[1] for item in both], both[0][4][:8, :128]
    )
    pre_seven, out_seven = jnp.concatenate(pre_seven), jnp.concatenate(out_seven)
    pre_seven, out_seven, dlogits = settle(pre_seven, out_seven, dlogits)
    loss_part = both[0][3] + both[1][3]
    hidden = jnp.concatenate(hiddens)

    delta_seven = layer_delta(pre_seven, against_rows(dlogits, kept_eight))

    def upstream(delta, step):
        return against_rows(delta, kept_seven[step * width : (step + 1) * width])

    top_bit = bits[0]
    cuts = [0] + [batch_rows // 64 * mark for mark in (8, 27, 46)] + [batch_rows]

    def near_sums(first, delta):
        ups = {step: upstream(delta, step) for step in range(first, first + top_bit)}
        for bit in reversed(bits[1:]):
            for step in range(first, first + top_bit, 2 * bit):
                ups[step] = ups[step] + swap(ups[step + bit], "mp", bit)
        return ups[first]

    crossing = near_sums(top_bit, delta_seven)
    grad_eight = contract_rows(out_seven, dlogits)
    limit_eight, peak_eight = grad_limits(grad_eight, outs)
    crossing, grad_eight, limit_eight, peak_eight, delta_seven, dlogits = settle(
        crossing, grad_eight, limit_eight, peak_eight, delta_seven, dlogits
    )
    crossing = [crossing[low:high] for low, high in zip(cuts[:-1], cuts[1:])]
    crossed = [swap(crossing[0], "mp", top_bit)]
    grad_seven = contract_rows(hidden, delta_seven)
    limit_seven, peak_seven = grad_limits(grad_seven, width)
    tops = fold(jnp.stack([peak_eight, peak_seven]), jnp.maximum, ("dp",))
    crossing, crossed, grad_seven, limit_seven, tops, delta_seven = settle(
        crossing, crossed, grad_seven, limit_seven, tops, delta_seven
    )
    top_eight, top_seven = tops[0], tops[1]

    def cross(step):
        def work(carried):
            delta, crossing, crossed, own_up = carried
            if step == 0:
                own_up = near_sums(0, delta)
            return (delta, crossing, crossed + [swap(crossing[step + 1], "mp", top_bit)], own_up)

        return work

    def grad_fc_six(carried):
        _, _, crossed, own_up = carried
        delta_six = layer_delta(pre_six, own_up + jnp.concatenate(crossed))
        grad_six = contract_rows(inputs, delta_six)
        limit_six, peak_six = grad_limits(grad_six, width)
        return (delta_six, grad_six, limit_six, peak_six)

    def sum_or_max(one, two):
        return jnp.concatenate([one[:-1] + two[:-1], jnp.maximum(one[-1:], two[-1:])])

    def small_sums(carried):
        delta_six, grad_six, limit_six, peak_six = carried
        columns = [
            jnp.sum(item.astype(jnp.float32), axis=0) for item in (delta_six, delta_seven, dlogits)
        ]
        small = fold(jnp.concatenate(columns + [peak_six[None]]), sum_or_max, ("dp",))
        return (grad_six, limit_six, small)

    beside = [
        cross(0),
        cross(1),
        cross(2),
        grad_fc_six,
    ]
    (reduced_eight, reduced_seven), carried = scatter(
        [grad_eight.reshape(replicas, rows_eight, padded), grad_seven.reshape(replicas, rows_seven, width)],
        [limit_eight, limit_seven],
        [top_eight, top_seven],
        [noise_wide.reshape(replicas, rows_eight, padded), noise_seven.reshape(replicas, rows_seven, width)],
        [None, group_seven],
        [0, 0],
        False,
        beside,
        (delta_seven, crossing, crossed, None),
    )
    grad_six, limit_six, small = small_sums(carried)
    top_six = small[-1]
    (reduced_six,), (reduced_seven, reduced_eight) = scatter(
        [grad_six.reshape(replicas, rows_six, width)],
        [limit_six],
        [top_six],
        [noise_six.reshape(replicas, rows_six, width)],
        [group_six],
        [near_six],
        False,
        [same] * rings + [lambda carried: (carried[0], carried[1].T)],
        (reduced_seven, reduced_eight[:, :outs]),
    )
    grad_pair = small[: 2 * width].reshape(2, width)
    grad_out = small[2 * width : 2 * width + outs]
    squares = (
        jnp.sum(reduced_six * reduced_six)
        + jnp.sum(reduced_seven * reduced_seven)
        + jnp.sum(reduced_eight * reduced_eight)
        + jnp.sum(grad_pair * grad_pair) / replicas
        + jnp.sum(grad_out * grad_out) / (replicas * ways)
    )
    totals = fold(jnp.stack([squares, loss_part]), jnp.add, ("dp", "mp"))
    total_squares, loss = totals[0], totals[1]
    grad_norm = jnp.sqrt(total_squares)
    factor = clip_norm / jnp.maximum(grad_norm, clip_norm)
    new_six, new_m_six, new_v_six = adam_step(
        w_six, m_six, v_six, factor * reduced_six, decay_rate, learn_rate
    )
    new_seven, new_m_seven, new_v_seven = adam_step(
        w_seven, m_seven, v_seven, factor * reduced_seven, decay_rate, learn_rate
    )
    new_eight, new_m_eight, new_v_eight = (
        item.T
        for item in adam_step(
            w_eight.T, m_eight.T, v_eight.T, factor * reduced_eight, decay_rate, learn_rate
        )
    )
    new_biases, new_m_biases, new_v_biases = adam_step(
        biases, m_biases, v_biases, factor * grad_pair, 0.0, bias_rate
    )
    new_bias_out, new_m_bias_out, new_v_bias_out = adam_step(
        bias_out, m_bias_out, v_bias_out, factor * grad_out, 0.0, bias_rate
    )
    return (
        loss,
        grad_norm,
        new_six,
        new_seven,
        new_eight,
        new_m_six,
        new_m_seven,
        new_m_eight,
        new_v_six,
        new_v_seven,
        new_v_eight,
        new_six.astype(jnp.bfloat16),
        new_seven.astype(jnp.bfloat16),
        new_eight.astype(jnp.bfloat16),
        new_biases,
        new_bias_out,
        new_m_biases,
        new_v_biases,
        new_m_bias_out,
        new_v_bias_out,
    )


def solution(mesh):
    return jax.shard_map(
        shards,
        mesh=mesh,
        in_specs=(
            P("dp", "mp"),
            P("dp"),
            P("dp", "mp"),
            P("dp", "mp"),
            P(("dp", "mp"), None),
            P("dp", "mp"),
            P("dp", "mp"),
            P(("mp", "dp"), None),
            P("dp", "mp"),
            P("dp", "mp"),
            P(("mp", "dp"), None),
            P("dp", "mp"),
            P("dp", "mp"),
            P(("mp", "dp"), None),
            P(None, "mp"),
            P(),
            P(None, "mp"),
            P(None, "mp"),
            P(),
            P(),
        ),
        out_specs=(
            P(),
            P(),
            P("dp", "mp"),
            P("dp", "mp"),
            P(("mp", "dp"), None),
            P("dp", "mp"),
            P("dp", "mp"),
            P(("mp", "dp"), None),
            P("dp", "mp"),
            P("dp", "mp"),
            P(("mp", "dp"), None),
            P("dp", "mp"),
            P("dp", "mp"),
            P(("mp", "dp"), None),
            P(None, "mp"),
            P(),
            P(None, "mp"),
            P(None, "mp"),
            P(),
            P(),
        ),
        check_vma=False,
    )
```
